256 devices in a mesh: dp: 8 (over x, core), seq: 32 (over z, y).
Axes of the slice: x: 4, y: 4, z: 8, core: 2. Of those that a mesh axis runs over, the one named last changes fastest.
Arguments:
- x_rows: bfloat16 [8, 2048, 4096], P('dp', 'seq'), may hold values from -6 to 6
- router_weight: float32 [4096], replicated, may hold values from -0.09375 to 0.09375
- query_rows: bfloat16 [8, 2048, 4096], P('dp', 'seq'), may hold values from -8 to 8
- key_rows: bfloat16 [8, 2048, 4096], P('dp', 'seq'), may hold values from -8 to 8
- value_rows: bfloat16 [8, 2048, 4096], P('dp', 'seq'), may hold values from -6 to 6
- cotangent: bfloat16 [8, 2048, 4096], P('dp', 'seq'), may hold values from -6 to 6
- picked: int32 [8, 2048], P('dp', 'seq'), may hold values from -1 to 511, as said below
- dest_owner: int32 [8, 2048], P('dp', 'seq'), may hold values from -1 to 31, as said below
- dest_slot: int32 [8, 2048], P('dp', 'seq'), may hold values from -1 to 31, as said below
Outputs:
- blended: bfloat16 [8, 2048, 4096], P('dp', 'seq')
- grad_queries: bfloat16 [8, 2048, 4096], P('dp', 'seq')
- grad_keys: bfloat16 [8, 2048, 4096], P('dp', 'seq')
- grad_values: bfloat16 [8, 2048, 4096], P('dp', 'seq')
- logit_grad: float32 [8, 2048], P('dp', 'seq')
- router_grad: float32 [4096], replicated
The draws below stay inside these ranges and needn't reach their ends.
Inputs may be any that keep to these rules, and one draw needn't show every extreme that they name: `picked`: in each shard the live slots come first and hold distinct token indices in increasing order; a shard has at most 64 live slots and in every sequence some shard has exactly 64; the live slots of a sequence number 1024; empty slots hold -1. Over a sequence's live slots the pairs (dest_owner, dest_slot) name each of the 32 x 32 places exactly once; no shard sends more than 2 rows to one owner, and some shard sends exactly 2; -1 at empty slots. `dest_slot`: see dest_owner; -1 at empty slots.
All inputs are finite; a program needn't handle non-finite values.
Results may differ from the reference program's by a relative error of at most 0.017.
Values may be sent and summed in bfloat16 or wider, within the bound.
A program may use at most 64 MiB of HBM per device.

```python
import jax
import jax.numpy as jnp
from jax import lax

HEADS = 32
HEAD_DIM = 128
D = 4096
BAL = 32
TOK_DEV = 512
CAP = 64
BATCH = 8
N_DP = 8
N_SEQ = 32


def index_tables(key):

    def one_sequence(subkey):
        key_a, key_b, key_c, key_d = jax.random.split(subkey, 4)
        order = jax.random.permutation(key_a, N_SEQ)
        shift = jax.random.randint(key_b, (N_SEQ // 2,), 0, BAL + 1).astype(jnp.int32)
        shift = shift.at[0].set(BAL)
        counts = jnp.zeros((N_SEQ,), jnp.int32).at[order[0::2]].set(BAL + shift).at[order[1::2]].set(BAL - shift)
        spots = jax.vmap(lambda inner: jax.random.permutation(inner, TOK_DEV)[:CAP])(jax.random.split(key_c, N_SEQ)).astype(jnp.int32)
        lane = jnp.arange(CAP, dtype=jnp.int32)
        live = lane[None, :] < counts[:, None]
        chosen = jnp.sort(jnp.where(live, spots, TOK_DEV), axis=1)
        picks = jnp.where(live, chosen, -1)
        start = jnp.cumsum(counts) - counts
        rank = start[:, None] + lane[None, :]
        sigma = jax.random.permutation(key_d, N_SEQ).astype(jnp.int32)
        owners = jnp.where(live, sigma[rank % N_SEQ], -1)
        slots = jnp.where(live, rank // N_SEQ, -1)
        return (picks.reshape(-1), owners.reshape(-1).astype(jnp.int32), slots.reshape(-1).astype(jnp.int32))
    return jax.vmap(one_sequence)(jax.random.split(key, N_DP))


def draw_picked(key, part):
    return index_tables(key)[0]


def draw_dest_owner(key, part):
    return index_tables(key)[1]


def draw_dest_slot(key, part):
    return index_tables(key)[2]


def draw_query_rows(key, part):
    key = jax.random.fold_in(key, 11)
    bulk = jnp.clip(jax.random.normal(key, (N_DP, N_SEQ, CAP, D), jnp.float32), -6.0, 6.0)
    return bulk.reshape(N_DP, N_SEQ * CAP, D).astype(jnp.bfloat16)


def draw_key_rows(key, part):
    key = jax.random.fold_in(key, 13)
    bulk = jnp.clip(jax.random.normal(key, (N_DP, N_SEQ, CAP, D), jnp.float32), -6.0, 6.0)
    return bulk.reshape(N_DP, N_SEQ * CAP, D).astype(jnp.bfloat16)


def steps_of(stream_key, extent, pieces, least, top_value):
    loudness, own = 1.0, jax.random.fold_in(stream_key, 6)
    for axis_at, parts in pieces:
        steps = jnp.exp(jax.random.uniform(jax.random.fold_in(own, axis_at), (parts,), jnp.float32, least / len(pieces), top_value / len(pieces)))
        loudness = loudness * jnp.repeat(steps, extent[axis_at] // parts).reshape([-1 if axis == axis_at else 1 for axis in range(len(extent))])
    return loudness


def noise(rng, extent, width, reach, pieces=(), kind=jnp.bfloat16):
    result = jax.random.normal(rng, extent, jnp.float32) * width
    if len(pieces) > 0:
        result = steps_of(rng, extent, pieces, -0.22, 0.18) * result
    return jnp.clip(result, min=-reach, max=reach).astype(kind)


def setup_inputs(seed: int = 0) -> dict:
    keys = jax.random.split(jax.random.key(seed), 10)
    x_rows = noise(keys[0], (BATCH, N_SEQ * CAP, D), 1.0, 6.0, ((0, 8), (1, 32)))
    router_weight = noise(keys[1], (D,), D ** -0.5, 0.09375, (), jnp.float32)
    query_rows = draw_query_rows(jax.random.fold_in(keys[9], 71), 0)
    key_rows = draw_key_rows(jax.random.fold_in(keys[9], 71), 0)
    value_rows = noise(keys[4], (BATCH, N_SEQ * CAP, D), 1.0, 6.0, ((0, 8), (1, 32)))
    cotangent = noise(keys[5], (BATCH, N_SEQ * CAP, D), 1.0, 6.0, ((0, 8), (1, 32)))
    picked = draw_picked(jax.random.fold_in(keys[9], 71), 0)
    dest_owner = draw_dest_owner(jax.random.fold_in(keys[9], 71), 0)
    dest_slot = draw_dest_slot(jax.random.fold_in(keys[9], 71), 0)
    return {"x_rows": x_rows, "router_weight": router_weight, "query_rows": query_rows, "key_rows": key_rows, "value_rows": value_rows, "cotangent": cotangent, "picked": picked, "dest_owner": dest_owner, "dest_slot": dest_slot}


def head_pass(query, keyed, valued, grads, positions):
    scale = HEAD_DIM ** -0.5
    qf = query.astype(jnp.float32)
    kf = keyed.astype(jnp.float32)
    vf = valued.astype(jnp.float32)
    gf = grads.astype(jnp.float32)
    scores = jnp.dot(qf, kf.T) * scale
    allowed = positions[None, :] <= positions[:, None]
    scores = jnp.where(allowed, scores, -1e30)
    top = jnp.max(scores, axis=1, keepdims=True)
    expo = jnp.where(allowed, jnp.exp(scores - top), 0.0)
    probs = expo / jnp.sum(expo, axis=1, keepdims=True)
    weights = probs.astype(jnp.bfloat16)
    attn = jnp.dot(weights.astype(jnp.float32), vf).astype(jnp.bfloat16)
    dprob = jnp.dot(gf, vf.T)
    dscore = (probs * (dprob - jnp.sum(probs * dprob, axis=1, keepdims=True)) * scale).astype(jnp.bfloat16)
    dsf = dscore.astype(jnp.float32)
    grad_q = jnp.dot(dsf, kf).astype(jnp.bfloat16)
    grad_k = jnp.dot(dsf.T, qf).astype(jnp.bfloat16)
    grad_v = jnp.dot(weights.astype(jnp.float32).T, gf).astype(jnp.bfloat16)
    return jnp.stack([attn, grad_q, grad_k, grad_v], 0)


def reference(x_rows, router_weight, query_rows, key_rows, value_rows, cotangent, picked, dest_owner, dest_slot):
    total = N_SEQ * BAL

    def one_sequence(items):
        rows_x, query, keyed, valued, cotan, picks, owners, slots = items
        is_live = picks >= 0
        shard_of = jnp.arange(N_SEQ * CAP, dtype=jnp.int32) // CAP
        position = (shard_of * TOK_DEV + picks).astype(jnp.int32)
        logit = jnp.dot(rows_x.astype(jnp.float32), router_weight, precision=lax.Precision.HIGHEST)
        rate = jax.nn.sigmoid(logit)
        scaled_grad = (rate[:, None] * cotan.astype(jnp.float32)).astype(jnp.bfloat16)
        compact = jnp.where(is_live, owners * BAL + slots, total).astype(jnp.int32)
        stacked = jnp.stack([query, keyed, valued, scaled_grad], 1)
        dense = jnp.zeros((total, 4, D), jnp.bfloat16).at[compact].set(stacked, mode="drop")
        dense_pos = jnp.zeros((total,), jnp.int32).at[compact].set(position, mode="drop")
        per_head = dense.reshape(total, 4, HEADS, HEAD_DIM).transpose(2, 1, 0, 3)
        results = lax.map(lambda item: head_pass(item[0], item[1], item[2], item[3], dense_pos), per_head)
        full = results.transpose(2, 1, 0, 3).reshape(total, 4, D)
        back = full[jnp.minimum(compact, total - 1)]
        back = jnp.where(is_live[:, None, None], back, jnp.zeros((), jnp.bfloat16))
        attn = back[:, 0]
        blended = jnp.where(is_live[:, None], (rate[:, None] * attn.astype(jnp.float32)).astype(jnp.bfloat16), jnp.zeros((), jnp.bfloat16))
        dotted = jnp.sum(cotan.astype(jnp.float32) * attn.astype(jnp.float32), axis=1)
        logit_grad = jnp.where(is_live, dotted * rate * (1.0 - rate), jnp.zeros((), jnp.float32))
        partial_grad = jnp.dot(logit_grad, rows_x.astype(jnp.float32), precision=lax.Precision.HIGHEST)
        return blended, back[:, 1], back[:, 2], back[:, 3], logit_grad, partial_grad

    outs = lax.map(one_sequence, (x_rows, query_rows, key_rows, value_rows, cotangent, picked, dest_owner, dest_slot))
    return outs[0], outs[1], outs[2], outs[3], outs[4], jnp.sum(outs[5], axis=0)
```

```python
import functools

import jax
import jax.numpy as jnp
from jax import lax
from jax.experimental import pallas as pl
from jax.experimental.pallas import tpu as pltpu
from jax.sharding import PartitionSpec as P

HEAD_DIM = 128
MESH = pl.DeviceIdType.MESH
NEG = -1e30
LOG2E = 1.4426950408889634


def kernel(
    n_seq,
    n_dp,
    block,
    tile,
    x_hbm,
    w_ref,
    q_hbm,
    k_hbm,
    v_hbm,
    c_hbm,
    picked_ref,
    blend_out,
    dq_out,
    dk_out,
    dv_out,
    lg_ref,
    rg_ref,
    x_ref,
    c_ref,
    gs_ref,
    count_ref,
    counts,
    bias_ref,
    qs,
    ks,
    vs,
    gs,
    e_ref,
    o_ref,
    inv_ref,
    at_ref,
    dq_ref,
    dk_ref,
    dv_ref,
    gt_ref,
    qt_ref,
    home_ref,
    blend_ref,
    part_ref,
    part_in,
    dp_in,
    full_ref,
    in_send,
    in_recv,
    out_send,
    out_recv,
    sum_send,
    sum_recv,
    local_sem,
):
    cap = x_ref.shape[0]
    width = x_ref.shape[1]
    total = n_seq * cap
    me = lax.axis_index("seq")
    dp = lax.axis_index("dp")
    f32 = jnp.float32
    bf16 = jnp.bfloat16
    n_z, n_y = n_seq // 4, 4

    def peer_of(n):
        t = lax.rem(n, n_z)
        dz = lax.div(t + 1, 2) * (2 * lax.rem(t, 2) - 1) + n_z
        dy = lax.div(n, n_z)
        z = lax.rem(lax.div(me, n_y) + dz, n_z)
        y = lax.rem(lax.rem(me, n_y) + dy, n_y)
        return z * n_y + y

    def cols(p):
        return pl.ds(pl.multiple_of(p * HEAD_DIM, HEAD_DIM), HEAD_DIM)

    def rows(p):
        return pl.ds(pl.multiple_of(p * cap, cap), cap)

    load_x = pltpu.make_async_copy(x_hbm.at[0], x_ref, local_sem.at[0])
    load_c = pltpu.make_async_copy(c_hbm.at[0], c_ref, local_sem.at[1])
    load_x.start()
    load_c.start()

    barrier = pltpu.get_barrier_semaphore()

    @pl.loop(1, n_seq)
    def _(n):
        pl.semaphore_signal(barrier, inc=1, device_id={"seq": peer_of(n)}, device_id_type=MESH)

    @pl.loop(1, n_dp)
    def _(n):
        pl.semaphore_signal(
            barrier, inc=1, device_id={"dp": lax.rem(dp + n, n_dp)}, device_id_type=MESH
        )

    live_row = (picked_ref[...] >= 0).astype(f32)
    count = jnp.sum(live_row, axis=1, keepdims=True)
    count_ref[0] = jnp.broadcast_to(count, (1, HEAD_DIM))
    live = lax.broadcasted_iota(jnp.int32, (cap, 1), 0).astype(f32) < count
    pl.semaphore_wait(barrier, n_seq + n_dp - 2)

    def spread(src_of, dst, send, recv, own):
        @pl.loop(1, n_seq)
        def _(n):
            p = peer_of(n)
            pltpu.make_async_remote_copy(
                src_ref=src_of(p),
                dst_ref=dst,
                send_sem=send,
                recv_sem=recv,
                device_id={"seq": p},
                device_id_type=MESH,
            ).start()

        pltpu.make_async_copy(src_of(me), dst, own).start()

    spread(
        lambda p: count_ref, counts.at[pl.ds(me, 1)], in_send.at[4], in_recv.at[4], in_recv.at[4]
    )
    for a, (src, dst) in enumerate(((k_hbm, ks), (q_hbm, qs), (v_hbm, vs))):
        spread(
            lambda p, src=src: src.at[0, :, cols(p)],
            dst.at[rows(me), pl.ds(0, HEAD_DIM)],
            in_send.at[a],
            in_recv.at[a],
            in_recv.at[a],
        )

    load_x.wait()
    logit = jnp.sum(x_ref[...].astype(f32) * w_ref[...], axis=1, keepdims=True)
    rate = jax.nn.sigmoid(logit)
    load_c.wait()
    scaled = (rate * c_ref[...].astype(f32)).astype(bf16)
    gs_ref[...] = jnp.where(live, scaled.astype(f32), 0.0).astype(bf16)
    spread(
        lambda p: gs_ref.at[:, cols(p)], gs.at[rows(me)], in_send.at[3], in_recv.at[3], in_recv.at[3]
    )

    vs[:, HEAD_DIM:] = jnp.ones((total, HEAD_DIM), bf16)

    pltpu.make_async_copy(counts, counts, in_recv.at[4]).wait()
    lane = lax.broadcasted_iota(jnp.int32, (1, HEAD_DIM), 1).astype(f32)
    for t in range(total // HEAD_DIM):
        bound = jnp.where(lane < cap, counts[2 * t], counts[2 * t + 1] + cap)
        bias_ref[:, t * HEAD_DIM : (t + 1) * HEAD_DIM] = jnp.where(lane < bound, 0.0, NEG)

    def wait_all(ref, sem):
        pltpu.make_async_copy(ref, ref, sem).wait()

    scale = HEAD_DIM ** (-0.5)
    factor = scale * LOG2E
    n_blocks = total // block
    n_tiles = block // tile
    nt = (((1,), (1,)), ((), ()))

    def dot(a, b):
        return jnp.dot(a, b, preferred_element_type=f32)

    def dot_t(a, b):
        return lax.dot_general(a, b, nt, preferred_element_type=f32)

    wait_all(ks, in_recv.at[0])
    wait_all(qs, in_recv.at[1])

    for i in range(n_blocks):
        wide = (i + 1) * block

        @pl.loop(0, n_tiles)
        def _(r, i=i, wide=wide):
            here = pl.ds(pl.multiple_of(i * block + r * tile, tile), tile)
            s = dot_t(qs[here, :], ks[:wide, :]) * factor + bias_ref[:, :wide]
            diag = s[:, i * block :]
            row = lax.broadcasted_iota(jnp.int32, diag.shape, 0) + r * tile
            col = lax.broadcasted_iota(jnp.int32, diag.shape, 1)
            diag = jnp.where(col <= row, diag, NEG)
            top = jnp.max(diag, axis=1, keepdims=True)
            if i > 0:
                off = s[:, : i * block]
                top = jnp.maximum(top, jnp.max(off, axis=1, keepdims=True))
                e_ref[here, : i * block] = jnp.exp2(off - top).astype(bf16)
            e_ref[here, i * block : wide] = jnp.exp2(diag - top).astype(bf16)

    wait_all(vs.at[:, pl.ds(0, HEAD_DIM)], in_recv.at[2])

    for i in range(n_blocks):
        wide = (i + 1) * block

        @pl.loop(0, n_tiles)
        def _(r, i=i, wide=wide):
            here = pl.ds(pl.multiple_of(i * block + r * tile, tile), tile)
            both = dot(e_ref[here, :wide], vs[:wide, :])
            inv = 1.0 / both[:, HEAD_DIM:]
            out = both[:, :HEAD_DIM] * inv
            inv_ref[here, :] = inv
            o_ref[here, :] = out
            at_ref[here, :] = out.astype(bf16)

    def give_back(src, dst, send, recv):
        @pl.loop(1, n_seq)
        def _(n):
            p = peer_of(n)
            pltpu.make_async_remote_copy(
                src_ref=src.at[rows(p), :],
                dst_ref=dst.at[:, cols(me)],
                send_sem=send,
                recv_sem=recv,
                device_id={"seq": p},
                device_id_type=MESH,
            ).start()

        pltpu.make_async_copy(src.at[rows(me), :], dst.at[:, cols(me)], recv).start()

    give_back(at_ref, home_ref, out_send.at[0], out_recv.at[0])

    wait_all(gs, in_recv.at[3])

    @pl.loop(0, total // HEAD_DIM)
    def _(t):
        here = pl.ds(pl.multiple_of(t * HEAD_DIM, HEAD_DIM), HEAD_DIM)
        inv = inv_ref[here, :]
        gt_ref[:, here] = (gs[here, :].astype(f32) * inv).T.astype(bf16)
        qt_ref[:, here] = (qs[here, :].astype(f32) * (inv * scale)).T.astype(bf16)

    for j in range(n_blocks):
        lo = j * block
        res = dot(gt_ref[:, lo:], e_ref[lo:, lo : lo + block])
        dv_ref[lo : lo + block, :] = res.T.astype(bf16)
    give_back(dv_ref, dv_out.at[0], out_send.at[1], out_recv.at[1])

    for i in range(n_blocks):
        wide = (i + 1) * block

        @pl.loop(0, n_tiles)
        def _(r, i=i, wide=wide):
            here = pl.ds(pl.multiple_of(i * block + r * tile, tile), tile)
            g = gs[here, :]
            mean = jnp.sum(g.astype(f32) * o_ref[here, :], axis=1, keepdims=True)
            dprob = dot_t(g, vs[:wide, :HEAD_DIM])
            ds = (e_ref[here, :wide].astype(f32) * (dprob - mean)).astype(bf16)
            e_ref[here, :wide] = ds
            dq = dot(ds, ks[:wide, :]) * (inv_ref[here, :] * scale)
            dq_ref[here, :] = dq.astype(bf16)

    give_back(dq_ref, dq_out.at[0], out_send.at[2], out_recv.at[2])

    for j in range(n_blocks):
        lo = j * block
        res = dot(qt_ref[:, lo:], e_ref[lo:, lo : lo + block])
        dk_ref[lo : lo + block, :] = res.T.astype(bf16)
    give_back(dk_ref, dk_out.at[0], out_send.at[3], out_recv.at[3])

    wait_all(home_ref, out_recv.at[0])
    attn = home_ref[...].astype(f32)
    blend_ref[...] = jnp.where(live, rate * attn, 0.0).astype(bf16)
    store = pltpu.make_async_copy(blend_ref, blend_out.at[0], local_sem.at[2])
    store.start()
    dotted = jnp.sum(c_ref[...].astype(f32) * attn, axis=1, keepdims=True)
    lg = jnp.where(live, dotted * rate * (1.0 - rate), 0.0)
    eye = lax.broadcasted_iota(jnp.int32, (cap, cap), 0) == lax.broadcasted_iota(
        jnp.int32, (cap, cap), 1
    )
    lg_ref[...] = jnp.sum(jnp.where(eye, lg, 0.0), axis=0, keepdims=True)
    part = jnp.sum(lg * x_ref[...].astype(f32), axis=0, keepdims=True)
    for p in range(n_seq):
        part_ref[p] = part[:, p * HEAD_DIM : (p + 1) * HEAD_DIM]

    spread(
        lambda p: part_ref.at[pl.ds(p, 1)],
        part_in.at[pl.ds(me, 1)],
        sum_send.at[0],
        sum_recv.at[0],
        sum_recv.at[0],
    )
    wait_all(part_in, sum_recv.at[0])
    count_sum = jnp.sum(part_in[...], axis=0, keepdims=True)
    dp_in[pl.ds(dp, 1)] = count_sum

    @pl.loop(1, n_dp)
    def _(n):
        pltpu.make_async_remote_copy(
            src_ref=dp_in.at[pl.ds(dp, 1)],
            dst_ref=dp_in.at[pl.ds(dp, 1)],
            send_sem=sum_send.at[1],
            recv_sem=sum_recv.at[1],
            device_id={"dp": lax.rem(dp + n, n_dp)},
            device_id_type=MESH,
        ).start()

    wait_all(dp_in.at[pl.ds(0, n_dp - 1)], sum_recv.at[1])
    full_ref[pl.ds(me, 1)] = jnp.sum(dp_in[...], axis=0, keepdims=True)

    @pl.loop(1, n_seq)
    def _(n):
        pltpu.make_async_remote_copy(
            src_ref=full_ref.at[pl.ds(me, 1)],
            dst_ref=full_ref.at[pl.ds(me, 1)],
            send_sem=sum_send.at[2],
            recv_sem=sum_recv.at[2],
            device_id={"seq": peer_of(n)},
            device_id_type=MESH,
        ).start()

    wait_all(full_ref.at[pl.ds(0, n_seq - 1)], sum_recv.at[2])
    for p in range(n_seq):
        rg_ref[:, p * HEAD_DIM : (p + 1) * HEAD_DIM] = full_ref[p]

    store.wait()
    for a, dst in ((1, dv_out), (2, dq_out), (3, dk_out)):
        wait_all(dst, out_recv.at[a])
    sent = pl.ds(0, total - cap)
    for a in range(4):
        wait_all(ks.at[sent, :], in_send.at[a])
        wait_all(ks.at[sent, :], out_send.at[a])
    most = pl.ds(0, n_seq - 1)
    wait_all(counts.at[most], in_send.at[4])
    wait_all(counts.at[most], sum_send.at[0])
    wait_all(dp_in.at[pl.ds(0, n_dp - 1)], sum_send.at[1])
    wait_all(counts.at[most], sum_send.at[2])


def body(x_rows, router_weight, query_rows, key_rows, value_rows, cotangent, picked):
    n_seq = lax.axis_size("seq")
    n_dp = lax.axis_size("dp")
    _, cap, width = x_rows.shape
    total = n_seq * cap
    block = min(512, total // 2)
    tile = 128
    f32 = jnp.float32
    bf16 = jnp.bfloat16
    anyspace = pl.BlockSpec(memory_space=pl.ANY)
    vmem = pl.BlockSpec(memory_space=pltpu.VMEM)
    big = jax.ShapeDtypeStruct(x_rows.shape, bf16)
    head = pltpu.VMEM((total, HEAD_DIM), bf16)
    headf = pltpu.VMEM((total, HEAD_DIM), f32)
    own = pltpu.VMEM((cap, width), bf16)
    chunks = pltpu.VMEM((n_seq, 1, HEAD_DIM), f32)
    out = pl.pallas_call(
        functools.partial(kernel, n_seq, n_dp, block, tile),
        out_shape=(
            big,
            big,
            big,
            big,
            jax.ShapeDtypeStruct((1, cap), f32),
            jax.ShapeDtypeStruct((1, width), f32),
        ),
        in_specs=[anyspace, vmem, anyspace, anyspace, anyspace, anyspace, vmem],
        out_specs=(anyspace, anyspace, anyspace, anyspace, vmem, vmem),
        scratch_shapes=[
            own,
            own,
            own,
            pltpu.VMEM((1, 1, HEAD_DIM), f32),
            chunks,
            pltpu.VMEM((1, total), f32),
            head,
            head,
            pltpu.VMEM((total, 2 * HEAD_DIM), bf16),
            head,
            pltpu.VMEM((total, total), bf16),
            headf,
            headf,
            head,
            head,
            head,
            head,
            pltpu.VMEM((HEAD_DIM, total), bf16),
            pltpu.VMEM((HEAD_DIM, total), bf16),
            own,
            own,
            chunks,
            chunks,
            pltpu.VMEM((n_dp, 1, HEAD_DIM), f32),
            chunks,
            pltpu.SemaphoreType.DMA((5,)),
            pltpu.SemaphoreType.DMA((5,)),
            pltpu.SemaphoreType.DMA((4,)),
            pltpu.SemaphoreType.DMA((4,)),
            pltpu.SemaphoreType.DMA((3,)),
            pltpu.SemaphoreType.DMA((3,)),
            pltpu.SemaphoreType.DMA((3,)),
        ],
        compiler_params=pltpu.CompilerParams(
            collective_id=0, has_side_effects=True, vmem_limit_bytes=48 * 1024 * 1024
        ),
    )(
        x_rows,
        router_weight.reshape(1, width),
        query_rows,
        key_rows,
        value_rows,
        cotangent,
        picked,
    )
    blended, grad_q, grad_k, grad_v, logit_grad, router_grad = out
    return blended, grad_q, grad_k, grad_v, logit_grad, router_grad.reshape(width)


def solution(mesh):
    row3 = P("dp", "seq", None)
    row2 = P("dp", "seq")
    mapped = jax.shard_map(
        body,
        mesh=mesh,
        in_specs=(row3, P(), row3, row3, row3, row3, row2),
        out_specs=(row3, row3, row3, row3, row2, P()),
        check_vma=False,
    )

    def run(
        x_rows,
        router_weight,
        query_rows,
        key_rows,
        value_rows,
        cotangent,
        picked,
        dest_owner,
        dest_slot,
    ):
        return mapped(
            x_rows, router_weight, query_rows, key_rows, value_rows, cotangent, picked
        )

    return run
```

```python
import functools

import jax
import jax.numpy as jnp
from jax import lax
from jax.experimental import pallas as pl
from jax.experimental.pallas import tpu as pltpu
from jax.sharding import PartitionSpec as P

HEAD_DIM = 128
MESH = pl.DeviceIdType.MESH
NEG = -1e30
LOG2E = 1.4426950408889634


def kernel(
    n_seq,
    n_dp,
    block,
    tile,
    x_hbm,
    w_hbm,
    q_hbm,
    k_hbm,
    v_hbm,
    c_hbm,
    picked_hbm,
    blend_out,
    dq_out,
    dk_out,
    dv_out,
    lg_ref,
    rg_ref,
    x_ref,
    c_ref,
    w_ref,
    picked_ref,
    gs_ref,
    count_ref,
    counts,
    bias_ref,
    qs,
    ks,
    vs,
    gs,
    e_ref,
    o_ref,
    inv_ref,
    at_ref,
    dq_ref,
    dk_ref,
    dv_ref,
    gt_ref,
    qt_ref,
    home_ref,
    blend_ref,
    part_ref,
    part_in,
    dp_in,
    full_ref,
    in_send,
    in_recv,
    out_send,
    out_recv,
    sum_send,
    sum_recv,
    local_sem,
):
    cap = x_ref.shape[0]
    width = x_ref.shape[1]
    total = n_seq * cap
    me = lax.axis_index("seq")
    dp = lax.axis_index("dp")
    f32 = jnp.float32
    bf16 = jnp.bfloat16
    n_z, n_y = n_seq // 4, 4

    def peer_of(n):
        t = lax.rem(n, n_z)
        dz = lax.div(t + 1, 2) * (2 * lax.rem(t, 2) - 1) + n_z
        dy = lax.div(n, n_z)
        z = lax.rem(lax.div(me, n_y) + dz, n_z)
        y = lax.rem(lax.rem(me, n_y) + dy, n_y)
        return z * n_y + y

    def cols(p):
        return pl.ds(pl.multiple_of(p * HEAD_DIM, HEAD_DIM), HEAD_DIM)

    def rows(p):
        return pl.ds(pl.multiple_of(p * cap, cap), cap)

    load_x = pltpu.make_async_copy(x_hbm.at[0], x_ref, local_sem.at[0])
    load_c = pltpu.make_async_copy(c_hbm.at[0], c_ref, local_sem.at[1])
    load_w = pltpu.make_async_copy(w_hbm, w_ref, local_sem.at[3])
    load_picked = pltpu.make_async_copy(picked_hbm, picked_ref, local_sem.at[4])
    load_picked.start()
    load_w.start()
    load_x.start()
    load_c.start()

    barrier = pltpu.get_barrier_semaphore()

    @pl.loop(1, n_seq)
    def _(n):
        pl.semaphore_signal(barrier, inc=1, device_id={"seq": peer_of(n)}, device_id_type=MESH)

    @pl.loop(1, n_dp)
    def _(n):
        pl.semaphore_signal(
            barrier, inc=1, device_id={"dp": lax.rem(dp + n, n_dp)}, device_id_type=MESH
        )

    load_picked.wait()
    live_row = (picked_ref[...] >= 0).astype(f32)
    count = jnp.sum(live_row, axis=1, keepdims=True)
    count_ref[0] = jnp.broadcast_to(count, (1, HEAD_DIM))
    live = lax.broadcasted_iota(jnp.int32, (cap, 1), 0).astype(f32) < count
    pl.semaphore_wait(barrier, n_seq + n_dp - 2)

    def spread(src_of, dst, send, recv, own):
        @pl.loop(1, n_seq)
        def _(n):
            p = peer_of(n)
            pltpu.make_async_remote_copy(
                src_ref=src_of(p),
                dst_ref=dst,
                send_sem=send,
                recv_sem=recv,
                device_id={"seq": p},
                device_id_type=MESH,
            ).start()

        pltpu.make_async_copy(src_of(me), dst, own).start()

    for a, (src, dst) in enumerate(((k_hbm, ks), (q_hbm, qs), (v_hbm, vs))):
        spread(
            lambda p, src=src: src.at[0, :, cols(p)],
            dst.at[rows(me), pl.ds(0, HEAD_DIM)],
            in_send.at[a],
            in_recv.at[a],
            in_recv.at[a],
        )
        if a == 0:
            spread(
                lambda p: count_ref,
                counts.at[pl.ds(me, 1)],
                in_send.at[4],
                in_recv.at[4],
                in_recv.at[4],
            )

    load_x.wait()
    load_w.wait()
    logit = jnp.sum(x_ref[...].astype(f32) * w_ref[...], axis=1, keepdims=True)
    rate = jax.nn.sigmoid(logit)
    load_c.wait()
    scaled = (rate * c_ref[...].astype(f32)).astype(bf16)
    gs_ref[...] = jnp.where(live, scaled.astype(f32), 0.0).astype(bf16)
    spread(
        lambda p: gs_ref.at[:, cols(p)], gs.at[rows(me)], in_send.at[3], in_recv.at[3], in_recv.at[3]
    )

    vs[:, HEAD_DIM:] = jnp.ones((total, HEAD_DIM), bf16)

    pltpu.make_async_copy(counts, counts, in_recv.at[4]).wait()
    lane = lax.broadcasted_iota(jnp.int32, (1, HEAD_DIM), 1).astype(f32)
    for t in range(total // HEAD_DIM):
        bound = jnp.where(lane < cap, counts[2 * t], counts[2 * t + 1] + cap)
        bias_ref[:, t * HEAD_DIM : (t + 1) * HEAD_DIM] = jnp.where(lane < bound, 0.0, NEG)

    def wait_all(ref, sem):
        pltpu.make_async_copy(ref, ref, sem).wait()

    scale = HEAD_DIM ** (-0.5)
    factor = scale * LOG2E
    n_blocks = total // block
    n_tiles = block // tile
    nt = (((1,), (1,)), ((), ()))

    def dot(a, b):
        return jnp.dot(a, b, preferred_element_type=f32)

    def dot_t(a, b):
        return lax.dot_general(a, b, nt, preferred_element_type=f32)

    wait_all(ks, in_recv.at[0])
    wait_all(qs, in_recv.at[1])

    for i in range(n_blocks):
        wide = (i + 1) * block

        @pl.loop(0, n_tiles)
        def _(r, i=i, wide=wide):
            here = pl.ds(pl.multiple_of(i * block + r * tile, tile), tile)
            s = dot_t(qs[here, :], ks[:wide, :]) * factor + bias_ref[:, :wide]
            diag = s[:, i * block :]
            row = lax.broadcasted_iota(jnp.int32, diag.shape, 0) + r * tile
            col = lax.broadcasted_iota(jnp.int32, diag.shape, 1)
            diag = jnp.where(col <= row, diag, NEG)
            top = jnp.max(diag, axis=1, keepdims=True)
            if i > 0:
                off = s[:, : i * block]
                top = jnp.maximum(top, jnp.max(off, axis=1, keepdims=True))
                e_ref[here, : i * block] = jnp.exp2(off - top).astype(bf16)
            e_ref[here, i * block : wide] = jnp.exp2(diag - top).astype(bf16)

    wait_all(vs.at[:, pl.ds(0, HEAD_DIM)], in_recv.at[2])

    for i in range(n_blocks):
        wide = (i + 1) * block

        @pl.loop(0, n_tiles)
        def _(r, i=i, wide=wide):
            here = pl.ds(pl.multiple_of(i * block + r * tile, tile), tile)
            both = dot(e_ref[here, :wide], vs[:wide, :])
            inv = 1.0 / both[:, HEAD_DIM:]
            out = both[:, :HEAD_DIM] * inv
            inv_ref[here, :] = inv
            o_ref[here, :] = out
            at_ref[here, :] = out.astype(bf16)

    def give_back(src, dst, send, recv, first=0, last=n_seq):
        @pl.loop(max(first, 1), last)
        def _(n):
            p = peer_of(n)
            pltpu.make_async_remote_copy(
                src_ref=src.at[rows(p), :],
                dst_ref=dst.at[:, cols(me)],
                send_sem=send,
                recv_sem=recv,
                device_id={"seq": p},
                device_id_type=MESH,
            ).start()

        if first == 0:
            pltpu.make_async_copy(src.at[rows(me), :], dst.at[:, cols(me)], recv).start()

    give_back(at_ref, home_ref, out_send.at[0], out_recv.at[0])

    wait_all(gs, in_recv.at[3])

    @pl.loop(0, total // HEAD_DIM)
    def _(t):
        here = pl.ds(pl.multiple_of(t * HEAD_DIM, HEAD_DIM), HEAD_DIM)
        inv = inv_ref[here, :]
        gt_ref[:, here] = (gs[here, :].astype(f32) * inv).T.astype(bf16)
        qt_ref[:, here] = (qs[here, :].astype(f32) * (inv * scale)).T.astype(bf16)

    for j in range(n_blocks):
        lo = j * block
        res = dot(gt_ref[:, lo:], e_ref[lo:, lo : lo + block])
        dv_ref[lo : lo + block, :] = res.T.astype(bf16)
    give_back(dv_ref, dv_out.at[0], out_send.at[1], out_recv.at[1])

    for i in range(n_blocks):
        wide = (i + 1) * block

        @pl.loop(0, n_tiles)
        def _(r, i=i, wide=wide):
            here = pl.ds(pl.multiple_of(i * block + r * tile, tile), tile)
            g = gs[here, :]
            mean = jnp.sum(g.astype(f32) * o_ref[here, :], axis=1, keepdims=True)
            dprob = dot_t(g, vs[:wide, :HEAD_DIM])
            ds = (e_ref[here, :wide].astype(f32) * (dprob - mean)).astype(bf16)
            e_ref[here, :wide] = ds
            dq = dot(ds, ks[:wide, :]) * (inv_ref[here, :] * scale)
            dq_ref[here, :] = dq.astype(bf16)

    wait_all(home_ref, out_recv.at[0])
    attn = home_ref[...].astype(f32)
    blend_ref[...] = jnp.where(live, rate * attn, 0.0).astype(bf16)
    store = pltpu.make_async_copy(blend_ref, blend_out.at[0], local_sem.at[2])
    store.start()
    dotted = jnp.sum(c_ref[...].astype(f32) * attn, axis=1, keepdims=True)
    lg = jnp.where(live, dotted * rate * (1.0 - rate), 0.0)
    eye = lax.broadcasted_iota(jnp.int32, (cap, cap), 0) == lax.broadcasted_iota(
        jnp.int32, (cap, cap), 1
    )
    lg_ref[...] = jnp.sum(jnp.where(eye, lg, 0.0), axis=0, keepdims=True)
    part = jnp.sum(lg * x_ref[...].astype(f32), axis=0, keepdims=True)
    for p in range(n_seq):
        part_ref[p] = part[:, p * HEAD_DIM : (p + 1) * HEAD_DIM]

    spread(
        lambda p: part_ref.at[pl.ds(p, 1)],
        part_in.at[pl.ds(me, 1)],
        sum_send.at[0],
        sum_recv.at[0],
        sum_recv.at[0],
    )
    give_back(dq_ref, dq_out.at[0], out_send.at[2], out_recv.at[2])

    for j in range(n_blocks):
        lo = j * block
        res = dot(qt_ref[:, lo:], e_ref[lo:, lo : lo + block])
        dk_ref[lo : lo + block, :] = res.T.astype(bf16)
    wait_all(part_in, sum_recv.at[0])
    count_sum = jnp.sum(part_in[...], axis=0, keepdims=True)
    dp_in[pl.ds(dp, 1)] = count_sum

    @pl.loop(1, n_dp)
    def _(n):
        pltpu.make_async_remote_copy(
            src_ref=dp_in.at[pl.ds(dp, 1)],
            dst_ref=dp_in.at[pl.ds(dp, 1)],
            send_sem=sum_send.at[1],
            recv_sem=sum_recv.at[1],
            device_id={"dp": lax.rem(dp + n, n_dp)},
            device_id_type=MESH,
        ).start()

    give_back(dk_ref, dk_out.at[0], out_send.at[3], out_recv.at[3], 0, n_seq // 2)
    wait_all(dp_in.at[pl.ds(0, n_dp - 1)], sum_recv.at[1])
    full_ref[pl.ds(me, 1)] = jnp.sum(dp_in[...], axis=0, keepdims=True)

    @pl.loop(1, n_seq)
    def _(n):
        pltpu.make_async_remote_copy(
            src_ref=full_ref.at[pl.ds(me, 1)],
            dst_ref=full_ref.at[pl.ds(me, 1)],
            send_sem=sum_send.at[2],
            recv_sem=sum_recv.at[2],
            device_id={"seq": peer_of(n)},
            device_id_type=MESH,
        ).start()

    give_back(dk_ref, dk_out.at[0], out_send.at[3], out_recv.at[3], n_seq // 2, n_seq)

    wait_all(full_ref.at[pl.ds(0, n_seq - 1)], sum_recv.at[2])
    for p in range(n_seq):
        rg_ref[:, p * HEAD_DIM : (p + 1) * HEAD_DIM] = full_ref[p]

    store.wait()
    for a, dst in ((1, dv_out), (2, dq_out), (3, dk_out)):
        wait_all(dst, out_recv.at[a])
    sent = pl.ds(0, total - cap)
    for a in range(4):
        wait_all(ks.at[sent, :], in_send.at[a])
        wait_all(ks.at[sent, :], out_send.at[a])
    most = pl.ds(0, n_seq - 1)
    wait_all(counts.at[most], in_send.at[4])
    wait_all(counts.at[most], sum_send.at[0])
    wait_all(dp_in.at[pl.ds(0, n_dp - 1)], sum_send.at[1])
    wait_all(counts.at[most], sum_send.at[2])


def write_out(n, *refs):
    stage, (get, put) = refs[2 * n : 3 * n], refs[3 * n :]
    gets = [pltpu.make_async_copy(refs[a], stage[a], get.at[a]) for a in range(n)]
    puts = [pltpu.make_async_copy(stage[a], refs[n + a], put.at[a]) for a in range(n)]
    for copy in gets:
        copy.start()
    for a in range(n):
        gets[a].wait()
        puts[a].start()
    for copy in puts:
        copy.wait()


def body(x_rows, router_weight, query_rows, key_rows, value_rows, cotangent, picked):
    n_seq = lax.axis_size("seq")
    n_dp = lax.axis_size("dp")
    _, cap, width = x_rows.shape
    total = n_seq * cap
    block = min(512, total // 2)
    tile = 128
    f32 = jnp.float32
    bf16 = jnp.bfloat16
    anyspace = pl.BlockSpec(memory_space=pl.ANY)
    hbm = pl.BlockSpec(memory_space=pltpu.HBM)
    vmem = pl.BlockSpec(memory_space=pltpu.VMEM)
    big = jax.ShapeDtypeStruct(x_rows.shape, bf16)
    head = pltpu.VMEM((total, HEAD_DIM), bf16)
    headf = pltpu.VMEM((total, HEAD_DIM), f32)
    own = pltpu.VMEM((cap, width), bf16)
    chunks = pltpu.VMEM((n_seq, 1, HEAD_DIM), f32)
    out = pl.pallas_call(
        functools.partial(kernel, n_seq, n_dp, block, tile),
        out_shape=(
            big,
            big,
            big,
            big,
            jax.ShapeDtypeStruct((1, cap), f32),
            jax.ShapeDtypeStruct((1, width), f32),
        ),
        in_specs=[hbm] * 7,
        out_specs=(anyspace, anyspace, anyspace, anyspace, vmem, vmem),
        scratch_shapes=[
            own,
            own,
            pltpu.VMEM((1, width), f32),
            pltpu.VMEM((1, cap), jnp.int32),
            own,
            pltpu.VMEM((1, 1, HEAD_DIM), f32),
            chunks,
            pltpu.VMEM((1, total), f32),
            head,
            head,
            pltpu.VMEM((total, 2 * HEAD_DIM), bf16),
            head,
            pltpu.VMEM((total, total), bf16),
            headf,
            headf,
            head,
            head,
            head,
            head,
            pltpu.VMEM((HEAD_DIM, total), bf16),
            pltpu.VMEM((HEAD_DIM, total), bf16),
            own,
            own,
            chunks,
            chunks,
            pltpu.VMEM((n_dp, 1, HEAD_DIM), f32),
            chunks,
            pltpu.SemaphoreType.DMA((5,)),
            pltpu.SemaphoreType.DMA((5,)),
            pltpu.SemaphoreType.DMA((4,)),
            pltpu.SemaphoreType.DMA((4,)),
            pltpu.SemaphoreType.DMA((3,)),
            pltpu.SemaphoreType.DMA((3,)),
            pltpu.SemaphoreType.DMA((5,)),
        ],
        compiler_params=pltpu.CompilerParams(
            collective_id=0, has_side_effects=True, vmem_limit_bytes=61 * 1024 * 1024
        ),
    )(
        x_rows,
        router_weight.reshape(1, width),
        query_rows,
        key_rows,
        value_rows,
        cotangent,
        picked,
    )
    blended, grad_q, grad_k, grad_v, logit_grad, router_grad = pl.pallas_call(
        functools.partial(write_out, len(out)),
        out_shape=tuple(jax.ShapeDtypeStruct(o.shape, o.dtype) for o in out),
        in_specs=[anyspace] * len(out),
        out_specs=(hbm,) * len(out),
        scratch_shapes=[pltpu.VMEM(o.shape, o.dtype) for o in out]
        + [pltpu.SemaphoreType.DMA((len(out),))] * 2,
        compiler_params=pltpu.CompilerParams(vmem_limit_bytes=61 * 1024 * 1024),
    )(*out)
    return blended, grad_q, grad_k, grad_v, logit_grad, router_grad.reshape(width)


def solution(mesh):
    row3 = P("dp", "seq", None)
    row2 = P("dp", "seq")
    mapped = jax.shard_map(
        body,
        mesh=mesh,
        in_specs=(row3, P(), row3, row3, row3, row3, row2),
        out_specs=(row3, row3, row3, row3, row2, P()),
        check_vma=False,
    )

    def run(
        x_rows,
        router_weight,
        query_rows,
        key_rows,
        value_rows,
        cotangent,
        picked,
        dest_owner,
        dest_slot,
    ):
        return mapped(
            x_rows, router_weight, query_rows, key_rows, value_rows, cotangent, picked
        )

    return run
```

```python
import functools

import jax
import jax.numpy as jnp
from jax import lax
from jax.experimental import pallas as pl
from jax.experimental.pallas import tpu as pltpu
from jax.sharding import PartitionSpec as P

HEAD_DIM = 128
MESH = pl.DeviceIdType.MESH
NEG = -1e30
LOG2E = 1.4426950408889634


def kernel(
    n_seq,
    n_dp,
    block,
    tile,
    x_hbm,
    w_hbm,
    q_hbm,
    k_hbm,
    v_hbm,
    c_hbm,
    picked_hbm,
    blend_out,
    dq_out,
    dk_out,
    dv_out,
    lg_ref,
    rg_ref,
    x_ref,
    c_ref,
    w_ref,
    picked_ref,
    gs_ref,
    count_ref,
    counts,
    bias_ref,
    qs,
    ks,
    vs,
    gs,
    e_ref,
    o_ref,
    inv_ref,
    at_ref,
    dq_ref,
    dk_ref,
    dv_ref,
    gt_ref,
    qt_ref,
    home_ref,
    part_ref,
    part_in,
    dp_in,
    full_ref,
    in_send,
    in_recv,
    out_send,
    out_recv,
    sum_send,
    sum_recv,
    local_sem,
):
    cap = x_ref.shape[0]
    width = x_ref.shape[1]
    total = n_seq * cap
    me = lax.axis_index("seq")
    dp = lax.axis_index("dp")
    f32 = jnp.float32
    bf16 = jnp.bfloat16
    n_z, n_y = n_seq // 4, 4

    def peer_of(n):
        t = lax.rem(n, n_z)
        dz = lax.div(t + 1, 2) * (2 * lax.rem(t, 2) - 1) + n_z
        dy = lax.div(n, n_z)
        z = lax.rem(lax.div(me, n_y) + dz, n_z)
        y = lax.rem(lax.rem(me, n_y) + dy, n_y)
        return z * n_y + y

    def cols(p):
        return pl.ds(pl.multiple_of(p * HEAD_DIM, HEAD_DIM), HEAD_DIM)

    def rows(p):
        return pl.ds(pl.multiple_of(p * cap, cap), cap)

    load_x = pltpu.make_async_copy(x_hbm.at[0], x_ref, local_sem.at[0])
    load_c = pltpu.make_async_copy(c_hbm.at[0], c_ref, local_sem.at[1])
    load_w = pltpu.make_async_copy(w_hbm, w_ref, local_sem.at[2])
    load_picked = pltpu.make_async_copy(picked_hbm, picked_ref, local_sem.at[3])
    load_picked.start()
    load_w.start()
    load_x.start()
    load_c.start()

    barrier = pltpu.get_barrier_semaphore()

    @pl.loop(1, n_seq)
    def _(n):
        pl.semaphore_signal(barrier, inc=1, device_id={"seq": peer_of(n)}, device_id_type=MESH)

    @pl.loop(1, n_dp)
    def _(n):
        pl.semaphore_signal(
            barrier, inc=1, device_id={"dp": lax.rem(dp + n, n_dp)}, device_id_type=MESH
        )

    load_picked.wait()
    live_row = (picked_ref[...] >= 0).astype(f32)
    count = jnp.sum(live_row, axis=1, keepdims=True)
    count_ref[0] = jnp.broadcast_to(count, (1, HEAD_DIM))
    live = lax.broadcasted_iota(jnp.int32, (cap, 1), 0).astype(f32) < count
    pl.semaphore_wait(barrier, n_seq + n_dp - 2)

    def spread(src_of, dst, send, recv, own):
        @pl.loop(1, n_seq)
        def _(n):
            p = peer_of(n)
            pltpu.make_async_remote_copy(
                src_ref=src_of(p),
                dst_ref=dst,
                send_sem=send,
                recv_sem=recv,
                device_id={"seq": p},
                device_id_type=MESH,
            ).start()

        pltpu.make_async_copy(src_of(me), dst, own).start()

    for a, (src, dst) in enumerate(((k_hbm, ks), (q_hbm, qs), (v_hbm, vs))):
        spread(
            lambda p, src=src: src.at[0, :, cols(p)],
            dst.at[rows(me), pl.ds(0, HEAD_DIM)],
            in_send.at[a],
            in_recv.at[a],
            in_recv.at[a],
        )
        if a == 0:
            spread(
                lambda p: count_ref,
                counts.at[pl.ds(me, 1)],
                in_send.at[4],
                in_recv.at[4],
                in_recv.at[4],
            )

    load_x.wait()
    load_w.wait()
    logit = jnp.sum(x_ref[...].astype(f32) * w_ref[...], axis=1, keepdims=True)
    rate = jax.nn.sigmoid(logit)
    load_c.wait()
    scaled = (rate * c_ref[...].astype(f32)).astype(bf16)
    gs_ref[...] = jnp.where(live, scaled.astype(f32), 0.0).astype(bf16)
    spread(
        lambda p: gs_ref.at[:, cols(p)], gs.at[rows(me)], in_send.at[3], in_recv.at[3], in_recv.at[3]
    )

    vs[:, HEAD_DIM:] = jnp.ones((total, HEAD_DIM), bf16)

    pltpu.make_async_copy(counts, counts, in_recv.at[4]).wait()
    lane = lax.broadcasted_iota(jnp.int32, (1, HEAD_DIM), 1).astype(f32)
    for t in range(total // HEAD_DIM):
        bound = jnp.where(lane < cap, counts[2 * t], counts[2 * t + 1] + cap)
        bias_ref[:, t * HEAD_DIM : (t + 1) * HEAD_DIM] = jnp.where(lane < bound, 0.0, NEG)

    def wait_all(ref, sem):
        pltpu.make_async_copy(ref, ref, sem).wait()

    scale = HEAD_DIM ** (-0.5)
    factor = scale * LOG2E
    n_blocks = total // block
    n_tiles = block // tile
    nt = (((1,), (1,)), ((), ()))

    def dot(a, b):
        return jnp.dot(a, b, preferred_element_type=f32)

    def dot_t(a, b):
        return lax.dot_general(a, b, nt, preferred_element_type=f32)

    wait_all(ks, in_recv.at[0])
    wait_all(qs, in_recv.at[1])

    for i in range(n_blocks):
        wide = (i + 1) * block

        @pl.loop(0, n_tiles)
        def _(r, i=i, wide=wide):
            here = pl.ds(pl.multiple_of(i * block + r * tile, tile), tile)
            s = dot_t(qs[here, :], ks[:wide, :]) * factor + bias_ref[:, :wide]
            diag = s[:, i * block :]
            row = lax.broadcasted_iota(jnp.int32, diag.shape, 0) + r * tile
            col = lax.broadcasted_iota(jnp.int32, diag.shape, 1)
            diag = jnp.where(col <= row, diag, NEG)
            top = jnp.max(diag, axis=1, keepdims=True)
            if i > 0:
                off = s[:, : i * block]
                top = jnp.maximum(top, jnp.max(off, axis=1, keepdims=True))
                e_ref[here, : i * block] = jnp.exp2(off - top).astype(bf16)
            e_ref[here, i * block : wide] = jnp.exp2(diag - top).astype(bf16)

    wait_all(vs.at[:, pl.ds(0, HEAD_DIM)], in_recv.at[2])

    for i in range(n_blocks):
        wide = (i + 1) * block

        @pl.loop(0, n_tiles)
        def _(r, i=i, wide=wide):
            here = pl.ds(pl.multiple_of(i * block + r * tile, tile), tile)
            both = dot(e_ref[here, :wide], vs[:wide, :])
            inv = 1.0 / both[:, HEAD_DIM:]
            out = both[:, :HEAD_DIM] * inv
            inv_ref[here, :] = inv
            o_ref[here, :] = out
            at_ref[here, :] = out.astype(bf16)

    def give_back(src, dst, send, recv, first=0, last=n_seq):
        @pl.loop(max(first, 1), last)
        def _(n):
            p = peer_of(n)
            pltpu.make_async_remote_copy(
                src_ref=src.at[rows(p), :],
                dst_ref=dst.at[:, cols(me)],
                send_sem=send,
                recv_sem=recv,
                device_id={"seq": p},
                device_id_type=MESH,
            ).start()

        if first == 0:
            pltpu.make_async_copy(src.at[rows(me), :], dst.at[:, cols(me)], recv).start()

    give_back(at_ref, home_ref, out_send.at[0], out_recv.at[0])

    wait_all(gs, in_recv.at[3])

    @pl.loop(0, total // HEAD_DIM)
    def _(t):
        here = pl.ds(pl.multiple_of(t * HEAD_DIM, HEAD_DIM), HEAD_DIM)
        inv = inv_ref[here, :]
        gt_ref[:, here] = (gs[here, :].astype(f32) * inv).T.astype(bf16)
        qt_ref[:, here] = (qs[here, :].astype(f32) * (inv * scale)).T.astype(bf16)

    for j in range(n_blocks):
        lo = j * block
        res = dot(gt_ref[:, lo:], e_ref[lo:, lo : lo + block])
        dv_ref[lo : lo + block, :] = res.T.astype(bf16)
    give_back(dv_ref, dv_out.at[0], out_send.at[1], out_recv.at[1])

    for i in range(n_blocks):
        wide = (i + 1) * block

        @pl.loop(0, n_tiles)
        def _(r, i=i, wide=wide):
            here = pl.ds(pl.multiple_of(i * block + r * tile, tile), tile)
            g = gs[here, :]
            mean = jnp.sum(g.astype(f32) * o_ref[here, :], axis=1, keepdims=True)
            dprob = dot_t(g, vs[:wide, :HEAD_DIM])
            ds = (e_ref[here, :wide].astype(f32) * (dprob - mean)).astype(bf16)
            e_ref[here, :wide] = ds
            dq = dot(ds, ks[:wide, :]) * (inv_ref[here, :] * scale)
            dq_ref[here, :] = dq.astype(bf16)

    wait_all(home_ref, out_recv.at[0])
    attn = home_ref[...].astype(f32)
    blend_out[0] = jnp.where(live, rate * attn, 0.0).astype(bf16)
    dotted = jnp.sum(c_ref[...].astype(f32) * attn, axis=1, keepdims=True)
    lg = jnp.where(live, dotted * rate * (1.0 - rate), 0.0)
    eye = lax.broadcasted_iota(jnp.int32, (cap, cap), 0) == lax.broadcasted_iota(
        jnp.int32, (cap, cap), 1
    )
    lg_ref[...] = jnp.sum(jnp.where(eye, lg, 0.0), axis=0, keepdims=True)
    part = jnp.sum(lg * x_ref[...].astype(f32), axis=0, keepdims=True)
    for p in range(n_seq):
        part_ref[p] = part[:, p * HEAD_DIM : (p + 1) * HEAD_DIM]

    spread(
        lambda p: part_ref.at[pl.ds(p, 1)],
        part_in.at[pl.ds(me, 1)],
        sum_send.at[0],
        sum_recv.at[0],
        sum_recv.at[0],
    )
    give_back(dq_ref, dq_out.at[0], out_send.at[2], out_recv.at[2])

    for j in range(n_blocks):
        lo = j * block
        res = dot(qt_ref[:, lo:], e_ref[lo:, lo : lo + block])
        dk_ref[lo : lo + block, :] = res.T.astype(bf16)
    wait_all(part_in, sum_recv.at[0])
    count_sum = jnp.sum(part_in[...], axis=0, keepdims=True)
    dp_in[pl.ds(dp, 1)] = count_sum

    @pl.loop(1, n_dp)
    def _(n):
        pltpu.make_async_remote_copy(
            src_ref=dp_in.at[pl.ds(dp, 1)],
            dst_ref=dp_in.at[pl.ds(dp, 1)],
            send_sem=sum_send.at[1],
            recv_sem=sum_recv.at[1],
            device_id={"dp": lax.rem(dp + n, n_dp)},
            device_id_type=MESH,
        ).start()

    give_back(dk_ref, dk_out.at[0], out_send.at[3], out_recv.at[3], 0, n_seq // 2)
    wait_all(dp_in.at[pl.ds(0, n_dp - 1)], sum_recv.at[1])
    full_ref[pl.ds(me, 1)] = jnp.sum(dp_in[...], axis=0, keepdims=True)

    @pl.loop(1, n_seq)
    def _(n):
        pltpu.make_async_remote_copy(
            src_ref=full_ref.at[pl.ds(me, 1)],
            dst_ref=full_ref.at[pl.ds(me, 1)],
            send_sem=sum_send.at[2],
            recv_sem=sum_recv.at[2],
            device_id={"seq": peer_of(n)},
            device_id_type=MESH,
        ).start()

    give_back(dk_ref, dk_out.at[0], out_send.at[3], out_recv.at[3], n_seq // 2, n_seq)

    wait_all(full_ref.at[pl.ds(0, n_seq - 1)], sum_recv.at[2])
    for p in range(n_seq):
        rg_ref[:, p * HEAD_DIM : (p + 1) * HEAD_DIM] = full_ref[p]

    for a, dst in ((1, dv_out), (2, dq_out), (3, dk_out)):
        wait_all(dst, out_recv.at[a])
    sent = pl.ds(0, total - cap)
    for a in range(4):
        wait_all(ks.at[sent, :], in_send.at[a])
        wait_all(ks.at[sent, :], out_send.at[a])
    most = pl.ds(0, n_seq - 1)
    wait_all(counts.at[most], in_send.at[4])
    wait_all(counts.at[most], sum_send.at[0])
    wait_all(dp_in.at[pl.ds(0, n_dp - 1)], sum_send.at[1])
    wait_all(counts.at[most], sum_send.at[2])


def write_out(n, *refs):
    sems = refs[2 * n]
    copies = [pltpu.make_async_copy(refs[a], refs[n + a], sems.at[a]) for a in range(n)]
    for copy in copies:
        copy.start()
    for copy in copies:
        copy.wait()


def body(x_rows, router_weight, query_rows, key_rows, value_rows, cotangent, picked):
    n_seq = lax.axis_size("seq")
    n_dp = lax.axis_size("dp")
    _, cap, width = x_rows.shape
    total = n_seq * cap
    block = min(512, total // 2)
    tile = 128
    f32 = jnp.float32
    bf16 = jnp.bfloat16
    anyspace = pl.BlockSpec(memory_space=pl.ANY)
    hbm = pl.BlockSpec(memory_space=pltpu.HBM)
    vmem = pl.BlockSpec(memory_space=pltpu.VMEM)
    big = pltpu.VMEM(x_rows.shape, bf16)
    head = pltpu.VMEM((total, HEAD_DIM), bf16)
    headf = pltpu.VMEM((total, HEAD_DIM), f32)
    own = pltpu.VMEM((cap, width), bf16)
    chunks = pltpu.VMEM((n_seq, 1, HEAD_DIM), f32)
    out = pl.pallas_call(
        functools.partial(kernel, n_seq, n_dp, block, tile),
        out_shape=(
            big,
            big,
            big,
            big,
            pltpu.VMEM((1, cap), f32),
            pltpu.VMEM((1, width), f32),
        ),
        in_specs=[hbm] * 7,
        out_specs=(vmem,) * 6,
        scratch_shapes=[
            own,
            own,
            pltpu.VMEM((1, width), f32),
            pltpu.VMEM((1, cap), jnp.int32),
            own,
            pltpu.VMEM((1, 1, HEAD_DIM), f32),
            chunks,
            pltpu.VMEM((1, total), f32),
            head,
            head,
            pltpu.VMEM((total, 2 * HEAD_DIM), bf16),
            head,
            pltpu.VMEM((total, total), bf16),
            headf,
            headf,
            head,
            head,
            head,
            head,
            pltpu.VMEM((HEAD_DIM, total), bf16),
            pltpu.VMEM((HEAD_DIM, total), bf16),
            own,
            chunks,
            chunks,
            pltpu.VMEM((n_dp, 1, HEAD_DIM), f32),
            chunks,
            pltpu.SemaphoreType.DMA((5,)),
            pltpu.SemaphoreType.DMA((5,)),
            pltpu.SemaphoreType.DMA((4,)),
            pltpu.SemaphoreType.DMA((4,)),
            pltpu.SemaphoreType.DMA((3,)),
            pltpu.SemaphoreType.DMA((3,)),
            pltpu.SemaphoreType.DMA((4,)),
        ],
        compiler_params=pltpu.CompilerParams(
            collective_id=0, has_side_effects=True, vmem_limit_bytes=48 * 1024 * 1024
        ),
    )(
        *(
            pltpu.with_memory_space_constraint(a, pltpu.HBM)
            for a in (
                x_rows,
                router_weight.reshape(1, width),
                query_rows,
                key_rows,
                value_rows,
                cotangent,
                picked,
            )
        )
    )
    blended, grad_q, grad_k, grad_v, logit_grad, router_grad = pl.pallas_call(
        functools.partial(write_out, len(out)),
        out_shape=tuple(pltpu.HBM(o.shape, o.dtype) for o in out),
        in_specs=[vmem] * len(out),
        out_specs=(hbm,) * len(out),
        scratch_shapes=[pltpu.SemaphoreType.DMA((len(out),))],
        compiler_params=pltpu.CompilerParams(vmem_limit_bytes=16 * 1024 * 1024),
    )(*out)
    return blended, grad_q, grad_k, grad_v, logit_grad, router_grad.reshape(width)


def solution(mesh):
    row3 = P("dp", "seq", None)
    row2 = P("dp", "seq")
    mapped = jax.shard_map(
        body,
        mesh=mesh,
        in_specs=(row3, P(), row3, row3, row3, row3, row2),
        out_specs=(row3, row3, row3, row3, row2, P()),
        check_vma=False,
    )

    def run(
        x_rows,
        router_weight,
        query_rows,
        key_rows,
        value_rows,
        cotangent,
        picked,
        dest_owner,
        dest_slot,
    ):
        return mapped(
            x_rows, router_weight, query_rows, key_rows, value_rows, cotangent, picked
        )

    return run
```

```python
import functools

import jax
import jax.numpy as jnp
from jax import lax
from jax.experimental import pallas as pl
from jax.experimental.pallas import tpu as pltpu
from jax.sharding import PartitionSpec as P

HEAD_DIM = 128
MESH = pl.DeviceIdType.MESH
NEG = -1e30
LOG2E = 1.4426950408889634


def kernel(
    n_seq,
    n_dp,
    block,
    tile,
    x_hbm,
    w_hbm,
    q_hbm,
    k_hbm,
    v_hbm,
    c_hbm,
    picked_hbm,
    blend_out,
    dq_out,
    dk_out,
    dv_out,
    lg_ref,
    rg_ref,
    x_ref,
    c_ref,
    w_ref,
    picked_ref,
    gs_ref,
    count_ref,
    counts,
    bias_ref,
    qs,
    ks,
    vs,
    gs,
    e_ref,
    o_ref,
    inv_ref,
    at_ref,
    dq_ref,
    dk_ref,
    dv_ref,
    gt_ref,
    qt_ref,
    home_ref,
    part_ref,
    part_in,
    dp_in,
    full_ref,
    in_send,
    in_recv,
    out_send,
    out_recv,
    sum_send,
    sum_recv,
    local_sem,
):
    cap = x_ref.shape[0]
    width = x_ref.shape[1]
    total = n_seq * cap
    me = lax.axis_index("seq")
    dp = lax.axis_index("dp")
    f32 = jnp.float32
    bf16 = jnp.bfloat16
    n_z, n_y = n_seq // 4, 4

    def peer_of(n):
        t = lax.rem(n, n_z)
        dz = lax.div(t + 1, 2) * (2 * lax.rem(t, 2) - 1) + n_z
        dy = lax.div(n, n_z)
        z = lax.rem(lax.div(me, n_y) + dz, n_z)
        y = lax.rem(lax.rem(me, n_y) + dy, n_y)
        return z * n_y + y

    def cols(p):
        return pl.ds(pl.multiple_of(p * HEAD_DIM, HEAD_DIM), HEAD_DIM)

    def rows(p):
        return pl.ds(pl.multiple_of(p * cap, cap), cap)

    load_x = pltpu.make_async_copy(x_hbm.at[0], x_ref, local_sem.at[0])
    load_c = pltpu.make_async_copy(c_hbm.at[0], c_ref, local_sem.at[1])
    load_w = pltpu.make_async_copy(w_hbm, w_ref, local_sem.at[2])
    load_picked = pltpu.make_async_copy(picked_hbm, picked_ref, local_sem.at[3])
    load_picked.start()
    load_w.start()
    load_x.start()
    load_c.start()

    barrier = pltpu.get_barrier_semaphore()

    @pl.loop(1, n_seq)
    def _(n):
        pl.semaphore_signal(barrier, inc=1, device_id={"seq": peer_of(n)}, device_id_type=MESH)

    @pl.loop(1, n_dp)
    def _(n):
        pl.semaphore_signal(
            barrier, inc=1, device_id={"dp": lax.rem(dp + n, n_dp)}, device_id_type=MESH
        )

    load_picked.wait()
    live_row = (picked_ref[...] >= 0).astype(f32)
    count = jnp.sum(live_row, axis=1, keepdims=True)
    count_ref[0] = jnp.broadcast_to(count, (1, HEAD_DIM))
    live = lax.broadcasted_iota(jnp.int32, (cap, 1), 0).astype(f32) < count
    pl.semaphore_wait(barrier, n_seq + n_dp - 2)

    def spread(src_of, dst, send, recv, own):
        @pl.loop(1, n_seq)
        def _(n):
            p = peer_of(n_seq - n)
            pltpu.make_async_remote_copy(
                src_ref=src_of(p),
                dst_ref=dst,
                send_sem=send,
                recv_sem=recv,
                device_id={"seq": p},
                device_id_type=MESH,
            ).start()

        pltpu.make_async_copy(src_of(me), dst, own).start()

    for a, (src, dst) in enumerate(((k_hbm, ks), (q_hbm, qs), (v_hbm, vs))):
        spread(
            lambda p, src=src: src.at[0, :, cols(p)],
            dst.at[rows(me), pl.ds(0, HEAD_DIM)],
            in_send.at[a],
            in_recv.at[a],
            in_recv.at[a],
        )
        if a == 0:
            spread(
                lambda p: count_ref,
                counts.at[pl.ds(me, 1)],
                in_send.at[4],
                in_recv.at[4],
                in_recv.at[4],
            )

    load_x.wait()
    load_w.wait()
    logit = jnp.sum(x_ref[...].astype(f32) * w_ref[...], axis=1, keepdims=True)
    rate = jax.nn.sigmoid(logit)
    load_c.wait()
    scaled = (rate * c_ref[...].astype(f32)).astype(bf16)
    gs_ref[...] = jnp.where(live, scaled.astype(f32), 0.0).astype(bf16)
    spread(
        lambda p: gs_ref.at[:, cols(p)], gs.at[rows(me)], in_send.at[3], in_recv.at[3], in_recv.at[3]
    )

    vs[:, HEAD_DIM:] = jnp.ones((total, HEAD_DIM), bf16)

    pltpu.make_async_copy(counts, counts, in_recv.at[4]).wait()
    lane = lax.broadcasted_iota(jnp.int32, (1, HEAD_DIM), 1).astype(f32)
    for t in range(total // HEAD_DIM):
        bound = jnp.where(lane < cap, counts[2 * t], counts[2 * t + 1] + cap)
        bias_ref[:, t * HEAD_DIM : (t + 1) * HEAD_DIM] = jnp.where(lane < bound, 0.0, NEG)

    def wait_all(ref, sem):
        pltpu.make_async_copy(ref, ref, sem).wait()

    scale = HEAD_DIM ** (-0.5)
    factor = scale * LOG2E
    n_blocks = total // block
    n_tiles = block // tile
    nt = (((1,), (1,)), ((), ()))

    def dot(a, b):
        return jnp.dot(a, b, preferred_element_type=f32)

    def dot_t(a, b):
        return lax.dot_general(a, b, nt, preferred_element_type=f32)

    wait_all(ks, in_recv.at[0])
    wait_all(qs, in_recv.at[1])

    for i in range(n_blocks):
        wide = (i + 1) * block

        @pl.loop(0, n_tiles)
        def _(r, i=i, wide=wide):
            here = pl.ds(pl.multiple_of(i * block + r * tile, tile), tile)
            s = dot_t(qs[here, :], ks[:wide, :]) * factor + bias_ref[:, :wide]
            diag = s[:, i * block :]
            row = lax.broadcasted_iota(jnp.int32, diag.shape, 0) + r * tile
            col = lax.broadcasted_iota(jnp.int32, diag.shape, 1)
            diag = jnp.where(col <= row, diag, NEG)
            top = jnp.max(diag, axis=1, keepdims=True)
            if i > 0:
                off = s[:, : i * block]
                top = jnp.maximum(top, jnp.max(off, axis=1, keepdims=True))
                e_ref[here, : i * block] = jnp.exp2(off - top).astype(bf16)
            e_ref[here, i * block : wide] = jnp.exp2(diag - top).astype(bf16)

    wait_all(vs.at[:, pl.ds(0, HEAD_DIM)], in_recv.at[2])

    for i in range(n_blocks):
        wide = (i + 1) * block

        @pl.loop(0, n_tiles)
        def _(r, i=i, wide=wide):
            here = pl.ds(pl.multiple_of(i * block + r * tile, tile), tile)
            both = dot(e_ref[here, :wide], vs[:wide, :])
            inv = 1.0 / both[:, HEAD_DIM:]
            out = both[:, :HEAD_DIM] * inv
            inv_ref[here, :] = inv
            o_ref[here, :] = out
            at_ref[here, :] = out.astype(bf16)

    def give_back(src, dst, send, recv, first=0, last=n_seq):
        @pl.loop(max(first, 1), last)
        def _(n):
            p = peer_of(n_seq - n)
            pltpu.make_async_remote_copy(
                src_ref=src.at[rows(p), :],
                dst_ref=dst.at[:, cols(me)],
                send_sem=send,
                recv_sem=recv,
                device_id={"seq": p},
                device_id_type=MESH,
            ).start()

        if first == 0:
            pltpu.make_async_copy(src.at[rows(me), :], dst.at[:, cols(me)], recv).start()

    give_back(at_ref, home_ref, out_send.at[0], out_recv.at[0])

    wait_all(gs, in_recv.at[3])

    @pl.loop(0, total // HEAD_DIM)
    def _(t):
        here = pl.ds(pl.multiple_of(t * HEAD_DIM, HEAD_DIM), HEAD_DIM)
        inv = inv_ref[here, :]
        gt_ref[:, here] = (gs[here, :].astype(f32) * inv).T.astype(bf16)
        qt_ref[:, here] = (qs[here, :].astype(f32) * (inv * scale)).T.astype(bf16)

    for j in range(n_blocks):
        lo = j * block
        res = dot(gt_ref[:, lo:], e_ref[lo:, lo : lo + block])
        dv_ref[lo : lo + block, :] = res.T.astype(bf16)
    give_back(dv_ref, dv_out.at[0], out_send.at[1], out_recv.at[1])

    for i in range(n_blocks):
        wide = (i + 1) * block

        @pl.loop(0, n_tiles)
        def _(r, i=i, wide=wide):
            here = pl.ds(pl.multiple_of(i * block + r * tile, tile), tile)
            g = gs[here, :]
            mean = jnp.sum(g.astype(f32) * o_ref[here, :], axis=1, keepdims=True)
            dprob = dot_t(g, vs[:wide, :HEAD_DIM])
            ds = (e_ref[here, :wide].astype(f32) * (dprob - mean)).astype(bf16)
            e_ref[here, :wide] = ds
            dq = dot(ds, ks[:wide, :]) * (inv_ref[here, :] * scale)
            dq_ref[here, :] = dq.astype(bf16)

    wait_all(home_ref, out_recv.at[0])
    attn = home_ref[...].astype(f32)
    blend_out[0] = jnp.where(live, rate * attn, 0.0).astype(bf16)
    dotted = jnp.sum(c_ref[...].astype(f32) * attn, axis=1, keepdims=True)
    lg = jnp.where(live, dotted * rate * (1.0 - rate), 0.0)
    eye = lax.broadcasted_iota(jnp.int32, (cap, cap), 0) == lax.broadcasted_iota(
        jnp.int32, (cap, cap), 1
    )
    lg_ref[...] = jnp.sum(jnp.where(eye, lg, 0.0), axis=0, keepdims=True)
    part = jnp.sum(lg * x_ref[...].astype(f32), axis=0, keepdims=True)
    for p in range(n_seq):
        part_ref[p] = part[:, p * HEAD_DIM : (p + 1) * HEAD_DIM]

    spread(
        lambda p: part_ref.at[pl.ds(p, 1)],
        part_in.at[pl.ds(me, 1)],
        sum_send.at[0],
        sum_recv.at[0],
        sum_recv.at[0],
    )
    give_back(dq_ref, dq_out.at[0], out_send.at[2], out_recv.at[2])

    for j in range(n_blocks):
        lo = j * block
        res = dot(qt_ref[:, lo:], e_ref[lo:, lo : lo + block])
        dk_ref[lo : lo + block, :] = res.T.astype(bf16)
    wait_all(part_in, sum_recv.at[0])
    count_sum = jnp.sum(part_in[...], axis=0, keepdims=True)
    dp_in[pl.ds(dp, 1)] = count_sum

    @pl.loop(1, n_dp)
    def _(n):
        pltpu.make_async_remote_copy(
            src_ref=dp_in.at[pl.ds(dp, 1)],
            dst_ref=dp_in.at[pl.ds(dp, 1)],
            send_sem=sum_send.at[1],
            recv_sem=sum_recv.at[1],
            device_id={"dp": lax.rem(dp + n, n_dp)},
            device_id_type=MESH,
        ).start()

    give_back(dk_ref, dk_out.at[0], out_send.at[3], out_recv.at[3], 0, n_seq // 2)
    wait_all(dp_in.at[pl.ds(0, n_dp - 1)], sum_recv.at[1])
    full_ref[pl.ds(me, 1)] = jnp.sum(dp_in[...], axis=0, keepdims=True)

    @pl.loop(1, n_seq)
    def _(n):
        pltpu.make_async_remote_copy(
            src_ref=full_ref.at[pl.ds(me, 1)],
            dst_ref=full_ref.at[pl.ds(me, 1)],
            send_sem=sum_send.at[2],
            recv_sem=sum_recv.at[2],
            device_id={"seq": peer_of(n)},
            device_id_type=MESH,
        ).start()

    give_back(dk_ref, dk_out.at[0], out_send.at[3], out_recv.at[3], n_seq // 2, n_seq)

    wait_all(full_ref.at[pl.ds(0, n_seq - 1)], sum_recv.at[2])
    for p in range(n_seq):
        rg_ref[:, p * HEAD_DIM : (p + 1) * HEAD_DIM] = full_ref[p]

    sent = pl.ds(0, total - cap)
    most = pl.ds(0, n_seq - 1)
    for a in range(4):
        wait_all(ks.at[sent, :], in_send.at[a])
    wait_all(counts.at[most], in_send.at[4])
    wait_all(counts.at[most], sum_send.at[0])
    wait_all(dp_in.at[pl.ds(0, n_dp - 1)], sum_send.at[1])
    wait_all(counts.at[most], sum_send.at[2])
    for a in range(3):
        wait_all(ks.at[sent, :], out_send.at[a])
    wait_all(dv_out, out_recv.at[1])
    wait_all(dq_out, out_recv.at[2])
    wait_all(ks.at[sent, :], out_send.at[3])
    wait_all(dk_out, out_recv.at[3])


def write_out(n, *refs):
    sems = refs[2 * n]
    copies = [pltpu.make_async_copy(refs[a], refs[n + a], sems.at[a]) for a in range(n)]
    for copy in copies:
        copy.start()
    for copy in copies:
        copy.wait()


def body(x_rows, router_weight, query_rows, key_rows, value_rows, cotangent, picked):
    n_seq = lax.axis_size("seq")
    n_dp = lax.axis_size("dp")
    _, cap, width = x_rows.shape
    total = n_seq * cap
    block = min(512, total // 2)
    tile = 128
    f32 = jnp.float32
    bf16 = jnp.bfloat16
    anyspace = pl.BlockSpec(memory_space=pl.ANY)
    hbm = pl.BlockSpec(memory_space=pltpu.HBM)
    vmem = pl.BlockSpec(memory_space=pltpu.VMEM)
    big = pltpu.VMEM(x_rows.shape, bf16)
    head = pltpu.VMEM((total, HEAD_DIM), bf16)
    headf = pltpu.VMEM((total, HEAD_DIM), f32)
    own = pltpu.VMEM((cap, width), bf16)
    chunks = pltpu.VMEM((n_seq, 1, HEAD_DIM), f32)
    out = pl.pallas_call(
        functools.partial(kernel, n_seq, n_dp, block, tile),
        out_shape=(
            big,
            big,
            big,
            big,
            pltpu.VMEM((1, cap), f32),
            pltpu.VMEM((1, width), f32),
        ),
        in_specs=[hbm] * 7,
        out_specs=(vmem,) * 6,
        scratch_shapes=[
            own,
            own,
            pltpu.VMEM((1, width), f32),
            pltpu.VMEM((1, cap), jnp.int32),
            own,
            pltpu.VMEM((1, 1, HEAD_DIM), f32),
            chunks,
            pltpu.VMEM((1, total), f32),
            head,
            head,
            pltpu.VMEM((total, 2 * HEAD_DIM), bf16),
            head,
            pltpu.VMEM((total, total), bf16),
            headf,
            headf,
            head,
            head,
            head,
            head,
            pltpu.VMEM((HEAD_DIM, total), bf16),
            pltpu.VMEM((HEAD_DIM, total), bf16),
            own,
            chunks,
            chunks,
            pltpu.VMEM((n_dp, 1, HEAD_DIM), f32),
            chunks,
            pltpu.SemaphoreType.DMA((5,)),
            pltpu.SemaphoreType.DMA((5,)),
            pltpu.SemaphoreType.DMA((4,)),
            pltpu.SemaphoreType.DMA((4,)),
            pltpu.SemaphoreType.DMA((3,)),
            pltpu.SemaphoreType.DMA((3,)),
            pltpu.SemaphoreType.DMA((4,)),
        ],
        compiler_params=pltpu.CompilerParams(
            collective_id=0, has_side_effects=True, vmem_limit_bytes=48 * 1024 * 1024
        ),
    )(
        *(
            pltpu.with_memory_space_constraint(a, pltpu.HBM)
            for a in (
                x_rows,
                router_weight.reshape(1, width),
                query_rows,
                key_rows,
                value_rows,
                cotangent,
                picked,
            )
        )
    )
    blended, grad_q, grad_k, grad_v, logit_grad, router_grad = pl.pallas_call(
        functools.partial(write_out, len(out)),
        out_shape=tuple(pltpu.HBM(o.shape, o.dtype) for o in out),
        in_specs=[vmem] * len(out),
        out_specs=(hbm,) * len(out),
        scratch_shapes=[pltpu.SemaphoreType.DMA((len(out),))],
        compiler_params=pltpu.CompilerParams(vmem_limit_bytes=16 * 1024 * 1024),
    )(*out)
    return blended, grad_q, grad_k, grad_v, logit_grad, router_grad.reshape(width)


def solution(mesh):
    row3 = P("dp", "seq", None)
    row2 = P("dp", "seq")
    mapped = jax.shard_map(
        body,
        mesh=mesh,
        in_specs=(row3, P(), row3, row3, row3, row3, row2),
        out_specs=(row3, row3, row3, row3, row2, P()),
        check_vma=False,
    )

    def run(
        x_rows,
        router_weight,
        query_rows,
        key_rows,
        value_rows,
        cotangent,
        picked,
        dest_owner,
        dest_slot,
    ):
        return mapped(
            x_rows, router_weight, query_rows, key_rows, value_rows, cotangent, picked
        )

    return run
```

```python
import functools

import jax
import jax.numpy as jnp
from jax import lax
from jax.experimental import pallas as pl
from jax.experimental.pallas import tpu as pltpu
from jax.sharding import PartitionSpec as P

HEAD_DIM = 128
MESH = pl.DeviceIdType.MESH
NEG = -1e30
LOG2E = 1.4426950408889634


def kernel(
    n_seq,
    n_dp,
    block,
    tile,
    x_hbm,
    w_hbm,
    q_hbm,
    k_hbm,
    v_hbm,
    c_hbm,
    picked_hbm,
    blend_out,
    dqk_out,
    dv_out,
    lg_ref,
    rg_ref,
    x_ref,
    c_ref,
    w_ref,
    picked_ref,
    gs_ref,
    count_ref,
    counts,
    bias_ref,
    stage_ref,
    kq,
    vs,
    gs,
    e_ref,
    o_ref,
    inv_ref,
    at_ref,
    dqk_ref,
    dv_ref,
    gt_ref,
    qt_ref,
    home_ref,
    part_ref,
    part_in,
    dp_in,
    full_ref,
    in_send,
    in_recv,
    out_send,
    out_recv,
    sum_send,
    sum_recv,
    local_sem,
):
    cap = x_ref.shape[0]
    width = x_ref.shape[1]
    total = n_seq * cap
    me = lax.axis_index("seq")
    dp = lax.axis_index("dp")
    f32 = jnp.float32
    bf16 = jnp.bfloat16
    n_z, n_y = n_seq // 4, 4

    def peer_of(n):
        t = lax.rem(n, n_z)
        dz = lax.div(t + 1, 2) * (2 * lax.rem(t, 2) - 1) + n_z
        dy = lax.div(n, n_z)
        z = lax.rem(lax.div(me, n_y) + dz, n_z)
        y = lax.rem(lax.rem(me, n_y) + dy, n_y)
        return z * n_y + y

    def cols(p):
        return pl.ds(pl.multiple_of(p * HEAD_DIM, HEAD_DIM), HEAD_DIM)

    def rows(p):
        return pl.ds(pl.multiple_of(p * cap, cap), cap)

    load_x = pltpu.make_async_copy(x_hbm.at[0], x_ref, local_sem.at[0])
    load_c = pltpu.make_async_copy(c_hbm.at[0], c_ref, local_sem.at[1])
    load_w = pltpu.make_async_copy(w_hbm, w_ref, local_sem.at[2])
    load_picked = pltpu.make_async_copy(picked_hbm, picked_ref, local_sem.at[3])
    load_k = pltpu.make_async_copy(k_hbm.at[0], stage_ref.at[0], local_sem.at[4])
    load_q = pltpu.make_async_copy(q_hbm.at[0], stage_ref.at[1], local_sem.at[5])
    load_picked.start()
    load_k.start()
    load_q.start()
    load_w.start()
    load_x.start()
    load_c.start()

    barrier = pltpu.get_barrier_semaphore()

    @pl.loop(1, n_seq)
    def _(n):
        pl.semaphore_signal(barrier, inc=1, device_id={"seq": peer_of(n)}, device_id_type=MESH)

    @pl.loop(1, n_dp)
    def _(n):
        pl.semaphore_signal(
            barrier, inc=1, device_id={"dp": lax.rem(dp + n, n_dp)}, device_id_type=MESH
        )

    load_picked.wait()
    live_row = (picked_ref[...] >= 0).astype(f32)
    count = jnp.sum(live_row, axis=1, keepdims=True)
    count_ref[0] = jnp.broadcast_to(count, (1, HEAD_DIM))
    live = lax.broadcasted_iota(jnp.int32, (cap, 1), 0).astype(f32) < count
    load_k.wait()
    load_q.wait()
    pl.semaphore_wait(barrier, n_seq + n_dp - 2)

    def spread(src_of, dst, send, recv, own):
        @pl.loop(1, n_seq)
        def _(n):
            p = peer_of(n_seq - n)
            pltpu.make_async_remote_copy(
                src_ref=src_of(p),
                dst_ref=dst,
                send_sem=send,
                recv_sem=recv,
                device_id={"seq": p},
                device_id_type=MESH,
            ).start()

        pltpu.make_async_copy(src_of(me), dst, own).start()

    spread(
        lambda p: stage_ref.at[:, :, cols(p)],
        kq.at[:, rows(me), :],
        in_send.at[0],
        in_recv.at[0],
        in_recv.at[0],
    )
    spread(
        lambda p: count_ref, counts.at[pl.ds(me, 1)], in_send.at[4], in_recv.at[4], in_recv.at[4]
    )
    spread(
        lambda p: v_hbm.at[0, :, cols(p)],
        vs.at[rows(me), pl.ds(0, HEAD_DIM)],
        in_send.at[2],
        in_recv.at[2],
        in_recv.at[2],
    )

    load_x.wait()
    load_w.wait()
    logit = jnp.sum(x_ref[...].astype(f32) * w_ref[...], axis=1, keepdims=True)
    rate = jax.nn.sigmoid(logit)
    load_c.wait()
    scaled = (rate * c_ref[...].astype(f32)).astype(bf16)
    gs_ref[...] = jnp.where(live, scaled.astype(f32), 0.0).astype(bf16)
    spread(
        lambda p: gs_ref.at[:, cols(p)], gs.at[rows(me)], in_send.at[3], in_recv.at[3], in_recv.at[3]
    )

    vs[:, HEAD_DIM:] = jnp.ones((total, HEAD_DIM), bf16)

    pltpu.make_async_copy(counts, counts, in_recv.at[4]).wait()
    lane = lax.broadcasted_iota(jnp.int32, (1, HEAD_DIM), 1).astype(f32)
    for t in range(total // HEAD_DIM):
        bound = jnp.where(lane < cap, counts[2 * t], counts[2 * t + 1] + cap)
        bias_ref[:, t * HEAD_DIM : (t + 1) * HEAD_DIM] = jnp.where(lane < bound, 0.0, NEG)

    def wait_all(ref, sem):
        pltpu.make_async_copy(ref, ref, sem).wait()

    scale = HEAD_DIM ** (-0.5)
    factor = scale * LOG2E
    n_blocks = total // block
    n_tiles = block // tile
    nt = (((1,), (1,)), ((), ()))

    def dot(a, b):
        return jnp.dot(a, b, preferred_element_type=f32)

    def dot_t(a, b):
        return lax.dot_general(a, b, nt, preferred_element_type=f32)

    wait_all(kq, in_recv.at[0])

    for i in range(n_blocks):
        wide = (i + 1) * block

        @pl.loop(0, n_tiles)
        def _(r, i=i, wide=wide):
            here = pl.ds(pl.multiple_of(i * block + r * tile, tile), tile)
            s = dot_t(kq[1, here, :], kq[0, :wide, :]) * factor + bias_ref[:, :wide]
            diag = s[:, i * block :]
            row = lax.broadcasted_iota(jnp.int32, diag.shape, 0) + r * tile
            col = lax.broadcasted_iota(jnp.int32, diag.shape, 1)
            diag = jnp.where(col <= row, diag, NEG)
            top = jnp.max(diag, axis=1, keepdims=True)
            if i > 0:
                off = s[:, : i * block]
                top = jnp.maximum(top, jnp.max(off, axis=1, keepdims=True))
                e_ref[here, : i * block] = jnp.exp2(off - top).astype(bf16)
            e_ref[here, i * block : wide] = jnp.exp2(diag - top).astype(bf16)

    wait_all(vs.at[:, pl.ds(0, HEAD_DIM)], in_recv.at[2])

    for i in range(n_blocks):
        wide = (i + 1) * block

        @pl.loop(0, n_tiles)
        def _(r, i=i, wide=wide):
            here = pl.ds(pl.multiple_of(i * block + r * tile, tile), tile)
            both = dot(e_ref[here, :wide], vs[:wide, :])
            inv = 1.0 / both[:, HEAD_DIM:]
            out = both[:, :HEAD_DIM] * inv
            inv_ref[here, :] = inv
            o_ref[here, :] = out
            at_ref[here, :] = out.astype(bf16)

    def give_back(src, dst, send, recv, first=0, last=n_seq):
        lead = (slice(None),) * (len(src.shape) - 2)

        @pl.loop(max(first, 1), last)
        def _(n):
            p = peer_of(n_seq - n)
            pltpu.make_async_remote_copy(
                src_ref=src.at[(*lead, rows(p), slice(None))],
                dst_ref=dst.at[(*lead, slice(None), cols(me))],
                send_sem=send,
                recv_sem=recv,
                device_id={"seq": p},
                device_id_type=MESH,
            ).start()

        if first == 0:
            pltpu.make_async_copy(
                src.at[(*lead, rows(me), slice(None))],
                dst.at[(*lead, slice(None), cols(me))],
                recv,
            ).start()

    give_back(at_ref, home_ref, out_send.at[0], out_recv.at[0])

    wait_all(gs, in_recv.at[3])

    @pl.loop(0, total // HEAD_DIM)
    def _(t):
        here = pl.ds(pl.multiple_of(t * HEAD_DIM, HEAD_DIM), HEAD_DIM)
        inv = inv_ref[here, :]
        gt_ref[:, here] = (gs[here, :].astype(f32) * inv).T.astype(bf16)
        qt_ref[:, here] = (kq[1, here, :].astype(f32) * (inv * scale)).T.astype(bf16)

    for j in range(n_blocks):
        lo = j * block
        res = dot(gt_ref[:, lo:], e_ref[lo:, lo : lo + block])
        dv_ref[lo : lo + block, :] = res.T.astype(bf16)
    give_back(dv_ref, dv_out.at[0], out_send.at[1], out_recv.at[1])

    for i in range(n_blocks):
        wide = (i + 1) * block

        @pl.loop(0, n_tiles)
        def _(r, i=i, wide=wide):
            here = pl.ds(pl.multiple_of(i * block + r * tile, tile), tile)
            g = gs[here, :]
            mean = jnp.sum(g.astype(f32) * o_ref[here, :], axis=1, keepdims=True)
            dprob = dot_t(g, vs[:wide, :HEAD_DIM])
            ds = (e_ref[here, :wide].astype(f32) * (dprob - mean)).astype(bf16)
            e_ref[here, :wide] = ds
            dq = dot(ds, kq[0, :wide, :]) * (inv_ref[here, :] * scale)
            dqk_ref[0, here, :] = dq.astype(bf16)

    for j in range(n_blocks):
        lo = j * block
        res = dot(qt_ref[:, lo:], e_ref[lo:, lo : lo + block])
        dqk_ref[1, lo : lo + block, :] = res.T.astype(bf16)
    wait_all(home_ref, out_recv.at[0])
    attn = home_ref[...].astype(f32)
    blend_out[0] = jnp.where(live, rate * attn, 0.0).astype(bf16)
    dotted = jnp.sum(c_ref[...].astype(f32) * attn, axis=1, keepdims=True)
    lg = jnp.where(live, dotted * rate * (1.0 - rate), 0.0)
    eye = lax.broadcasted_iota(jnp.int32, (cap, cap), 0) == lax.broadcasted_iota(
        jnp.int32, (cap, cap), 1
    )
    lg_ref[...] = jnp.sum(jnp.where(eye, lg, 0.0), axis=0, keepdims=True)
    part = jnp.sum(lg * x_ref[...].astype(f32), axis=0, keepdims=True)
    for p in range(n_seq):
        part_ref[p] = part[:, p * HEAD_DIM : (p + 1) * HEAD_DIM]

    spread(
        lambda p: part_ref.at[pl.ds(p, 1)],
        part_in.at[pl.ds(me, 1)],
        sum_send.at[0],
        sum_recv.at[0],
        sum_recv.at[0],
    )
    give_back(dqk_ref, dqk_out, out_send.at[2], out_recv.at[2], 0, n_seq // 3)

    wait_all(part_in, sum_recv.at[0])
    count_sum = jnp.sum(part_in[...], axis=0, keepdims=True)
    dp_in[pl.ds(dp, 1)] = count_sum

    @pl.loop(1, n_dp)
    def _(n):
        pltpu.make_async_remote_copy(
            src_ref=dp_in.at[pl.ds(dp, 1)],
            dst_ref=dp_in.at[pl.ds(dp, 1)],
            send_sem=sum_send.at[1],
            recv_sem=sum_recv.at[1],
            device_id={"dp": lax.rem(dp + n, n_dp)},
            device_id_type=MESH,
        ).start()

    give_back(dqk_ref, dqk_out, out_send.at[2], out_recv.at[2], n_seq // 3, 2 * n_seq // 3)
    wait_all(dp_in.at[pl.ds(0, n_dp - 1)], sum_recv.at[1])
    full_ref[pl.ds(me, 1)] = jnp.sum(dp_in[...], axis=0, keepdims=True)

    @pl.loop(1, n_seq)
    def _(n):
        pltpu.make_async_remote_copy(
            src_ref=full_ref.at[pl.ds(me, 1)],
            dst_ref=full_ref.at[pl.ds(me, 1)],
            send_sem=sum_send.at[2],
            recv_sem=sum_recv.at[2],
            device_id={"seq": peer_of(n)},
            device_id_type=MESH,
        ).start()

    give_back(dqk_ref, dqk_out, out_send.at[2], out_recv.at[2], 2 * n_seq // 3, n_seq)

    wait_all(full_ref.at[pl.ds(0, n_seq - 1)], sum_recv.at[2])
    for p in range(n_seq):
        rg_ref[:, p * HEAD_DIM : (p + 1) * HEAD_DIM] = full_ref[p]

    sent = pl.ds(0, total - cap)
    most = pl.ds(0, n_seq - 1)
    wait_all(kq.at[:, sent, :], in_send.at[0])
    wait_all(gs.at[sent, :], in_send.at[2])
    wait_all(gs.at[sent, :], in_send.at[3])
    wait_all(counts.at[most], in_send.at[4])
    wait_all(counts.at[most], sum_send.at[0])
    wait_all(dp_in.at[pl.ds(0, n_dp - 1)], sum_send.at[1])
    wait_all(counts.at[most], sum_send.at[2])
    wait_all(gs.at[sent, :], out_send.at[0])
    wait_all(gs.at[sent, :], out_send.at[1])
    wait_all(dv_out, out_recv.at[1])
    wait_all(kq.at[:, sent, :], out_send.at[2])
    wait_all(dqk_out, out_recv.at[2])


def write_out(blended, pair, grad_v, logit, router, o_b, o_q, o_k, o_v, o_l, o_r, sems):
    copies = [
        pltpu.make_async_copy(src, dst, sems.at[a])
        for a, (src, dst) in enumerate(
            (
                (blended, o_b),
                (pair.at[pl.ds(0, 1)], o_q),
                (pair.at[pl.ds(1, 1)], o_k),
                (grad_v, o_v),
                (logit, o_l),
                (router, o_r),
            )
        )
    ]
    for copy in copies:
        copy.start()
    for copy in copies:
        copy.wait()


def body(x_rows, router_weight, query_rows, key_rows, value_rows, cotangent, picked):
    n_seq = lax.axis_size("seq")
    n_dp = lax.axis_size("dp")
    _, cap, width = x_rows.shape
    total = n_seq * cap
    block = min(512, total // 2)
    tile = 128
    f32 = jnp.float32
    bf16 = jnp.bfloat16
    anyspace = pl.BlockSpec(memory_space=pl.ANY)
    hbm = pl.BlockSpec(memory_space=pltpu.HBM)
    vmem = pl.BlockSpec(memory_space=pltpu.VMEM)
    big = pltpu.VMEM(x_rows.shape, bf16)
    head = pltpu.VMEM((total, HEAD_DIM), bf16)
    headf = pltpu.VMEM((total, HEAD_DIM), f32)
    own = pltpu.VMEM((cap, width), bf16)
    chunks = pltpu.VMEM((n_seq, 1, HEAD_DIM), f32)
    out = pl.pallas_call(
        functools.partial(kernel, n_seq, n_dp, block, tile),
        out_shape=(
            big,
            pltpu.VMEM((2, cap, width), bf16),
            big,
            pltpu.VMEM((1, cap), f32),
            pltpu.VMEM((1, width), f32),
        ),
        in_specs=[hbm] * 7,
        out_specs=(vmem,) * 5,
        scratch_shapes=[
            own,
            own,
            pltpu.VMEM((1, width), f32),
            pltpu.VMEM((1, cap), jnp.int32),
            own,
            pltpu.VMEM((1, 1, HEAD_DIM), f32),
            chunks,
            pltpu.VMEM((1, total), f32),
            pltpu.VMEM((2, cap, width), bf16),
            pltpu.VMEM((2, total, HEAD_DIM), bf16),
            pltpu.VMEM((total, 2 * HEAD_DIM), bf16),
            head,
            pltpu.VMEM((total, total), bf16),
            headf,
            headf,
            head,
            pltpu.VMEM((2, total, HEAD_DIM), bf16),
            head,
            pltpu.VMEM((HEAD_DIM, total), bf16),
            pltpu.VMEM((HEAD_DIM, total), bf16),
            own,
            chunks,
            chunks,
            pltpu.VMEM((n_dp, 1, HEAD_DIM), f32),
            chunks,
            pltpu.SemaphoreType.DMA((5,)),
            pltpu.SemaphoreType.DMA((5,)),
            pltpu.SemaphoreType.DMA((4,)),
            pltpu.SemaphoreType.DMA((4,)),
            pltpu.SemaphoreType.DMA((3,)),
            pltpu.SemaphoreType.DMA((3,)),
            pltpu.SemaphoreType.DMA((6,)),
        ],
        compiler_params=pltpu.CompilerParams(
            collective_id=0, has_side_effects=True, vmem_limit_bytes=48 * 1024 * 1024
        ),
    )(
        *(
            pltpu.with_memory_space_constraint(a, pltpu.HBM)
            for a in (
                x_rows,
                router_weight.reshape(1, width),
                query_rows,
                key_rows,
                value_rows,
                cotangent,
                picked,
            )
        )
    )
    blended, grad_q, grad_k, grad_v, logit_grad, router_grad = pl.pallas_call(
        write_out,
        out_shape=(pltpu.HBM(x_rows.shape, bf16),) * 4
        + (pltpu.HBM((1, cap), f32), pltpu.HBM((1, width), f32)),
        in_specs=[vmem] * len(out),
        out_specs=(hbm,) * 6,
        scratch_shapes=[pltpu.SemaphoreType.DMA((6,))],
        compiler_params=pltpu.CompilerParams(vmem_limit_bytes=16 * 1024 * 1024),
    )(*out)
    return blended, grad_q, grad_k, grad_v, logit_grad, router_grad.reshape(width)


def solution(mesh):
    row3 = P("dp", "seq", None)
    row2 = P("dp", "seq")
    mapped = jax.shard_map(
        body,
        mesh=mesh,
        in_specs=(row3, P(), row3, row3, row3, row3, row2),
        out_specs=(row3, row3, row3, row3, row2, P()),
        check_vma=False,
    )

    def run(
        x_rows,
        router_weight,
        query_rows,
        key_rows,
        value_rows,
        cotangent,
        picked,
        dest_owner,
        dest_slot,
    ):
        return mapped(
            x_rows, router_weight, query_rows, key_rows, value_rows, cotangent, picked
        )

    return run
```

```python
import functools

import jax
import jax.numpy as jnp
from jax import lax
from jax.experimental import pallas as pl
from jax.experimental.pallas import tpu as pltpu
from jax.sharding import PartitionSpec as P

HEAD_DIM = 128
MESH = pl.DeviceIdType.MESH
NEG = -1e30
LOG2E = 1.4426950408889634


def kernel(
    n_seq,
    n_dp,
    block,
    tile,
    x_hbm,
    w_hbm,
    q_hbm,
    k_hbm,
    v_hbm,
    c_hbm,
    picked_hbm,
    blend_out,
    dq_out,
    dk_out,
    dv_out,
    lg_ref,
    rg_ref,
    x_ref,
    c_ref,
    w_ref,
    picked_ref,
    gs_ref,
    count_ref,
    counts,
    bias_ref,
    qs,
    ks,
    vs,
    gs,
    e_ref,
    o_ref,
    inv_ref,
    at_ref,
    dq_ref,
    dk_ref,
    dv_ref,
    gt_ref,
    qt_ref,
    home_ref,
    part_ref,
    part_in,
    dp_in,
    full_ref,
    in_send,
    in_recv,
    out_send,
    out_recv,
    sum_send,
    sum_recv,
    local_sem,
):
    cap = x_ref.shape[0]
    width = x_ref.shape[1]
    total = n_seq * cap
    me = lax.axis_index("seq")
    dp = lax.axis_index("dp")
    f32 = jnp.float32
    bf16 = jnp.bfloat16
    n_z, n_y = n_seq // 4, 4

    def peer_of(n):
        t = lax.rem(n, n_z)
        dz = lax.div(t + 1, 2) * (2 * lax.rem(t, 2) - 1) + n_z
        dy = lax.div(n, n_z)
        z = lax.rem(lax.div(me, n_y) + dz, n_z)
        y = lax.rem(lax.rem(me, n_y) + dy, n_y)
        return z * n_y + y

    def cols(p):
        return pl.ds(pl.multiple_of(p * HEAD_DIM, HEAD_DIM), HEAD_DIM)

    def rows(p):
        return pl.ds(pl.multiple_of(p * cap, cap), cap)

    load_x = pltpu.make_async_copy(x_hbm.at[0], x_ref, local_sem.at[0])
    load_c = pltpu.make_async_copy(c_hbm.at[0], c_ref, local_sem.at[1])
    load_w = pltpu.make_async_copy(w_hbm, w_ref, local_sem.at[2])
    load_picked = pltpu.make_async_copy(picked_hbm, picked_ref, local_sem.at[3])
    load_picked.start()
    load_w.start()
    load_x.start()
    load_c.start()

    barrier = pltpu.get_barrier_semaphore()

    @pl.loop(1, n_seq)
    def _(n):
        pl.semaphore_signal(barrier, inc=1, device_id={"seq": peer_of(n)}, device_id_type=MESH)

    @pl.loop(1, n_dp)
    def _(n):
        pl.semaphore_signal(
            barrier, inc=1, device_id={"dp": lax.rem(dp + n, n_dp)}, device_id_type=MESH
        )

    load_picked.wait()
    live_row = (picked_ref[...] >= 0).astype(f32)
    count = jnp.sum(live_row, axis=1, keepdims=True)
    count_ref[0] = jnp.broadcast_to(count, (1, HEAD_DIM))
    live = lax.broadcasted_iota(jnp.int32, (cap, 1), 0).astype(f32) < count
    pl.semaphore_wait(barrier, n_seq + n_dp - 2)

    def spread(src_of, dst, send, recv, own):
        @pl.loop(1, n_seq)
        def _(n):
            p = peer_of(n_seq - n)
            pltpu.make_async_remote_copy(
                src_ref=src_of(p),
                dst_ref=dst,
                send_sem=send,
                recv_sem=recv,
                device_id={"seq": p},
                device_id_type=MESH,
            ).start()

        pltpu.make_async_copy(src_of(me), dst, own).start()

    for a, (src, dst) in enumerate(((k_hbm, ks), (q_hbm, qs), (v_hbm, vs))):
        spread(
            lambda p, src=src: src.at[0, :, cols(p)],
            dst.at[rows(me), pl.ds(0, HEAD_DIM)],
            in_send.at[a],
            in_recv.at[a],
            in_recv.at[a],
        )
        if a == 0:
            spread(
                lambda p: count_ref,
                counts.at[pl.ds(me, 1)],
                in_send.at[4],
                in_recv.at[4],
                in_recv.at[4],
            )

    load_x.wait()
    load_w.wait()
    logit = jnp.sum(x_ref[...].astype(f32) * w_ref[...], axis=1, keepdims=True)
    rate = jax.nn.sigmoid(logit)
    load_c.wait()
    scaled = (rate * c_ref[...].astype(f32)).astype(bf16)
    gs_ref[...] = jnp.where(live, scaled.astype(f32), 0.0).astype(bf16)
    spread(
        lambda p: gs_ref.at[:, cols(p)], gs.at[rows(me)], in_send.at[3], in_recv.at[3], in_recv.at[3]
    )

    vs[:, HEAD_DIM:] = jnp.ones((total, HEAD_DIM), bf16)

    pltpu.make_async_copy(counts, counts, in_recv.at[4]).wait()
    lane = lax.broadcasted_iota(jnp.int32, (1, HEAD_DIM), 1).astype(f32)
    for t in range(total // HEAD_DIM):
        bound = jnp.where(lane < cap, counts[2 * t], counts[2 * t + 1] + cap)
        bias_ref[:, t * HEAD_DIM : (t + 1) * HEAD_DIM] = jnp.where(lane < bound, 0.0, NEG)

    def wait_all(ref, sem):
        pltpu.make_async_copy(ref, ref, sem).wait()

    scale = HEAD_DIM ** (-0.5)
    factor = scale * LOG2E
    n_blocks = total // block
    n_tiles = block // tile
    nt = (((1,), (1,)), ((), ()))

    def dot(a, b):
        return jnp.dot(a, b, preferred_element_type=f32)

    def dot_t(a, b):
        return lax.dot_general(a, b, nt, preferred_element_type=f32)

    wait_all(ks, in_recv.at[0])
    wait_all(qs, in_recv.at[1])

    for i in range(n_blocks):
        wide = (i + 1) * block

        @pl.loop(0, n_tiles)
        def _(r, i=i, wide=wide):
            here = pl.ds(pl.multiple_of(i * block + r * tile, tile), tile)
            s = dot_t(qs[here, :], ks[:wide, :]) * factor + bias_ref[:, :wide]
            diag = s[:, i * block :]
            row = lax.broadcasted_iota(jnp.int32, diag.shape, 0) + r * tile
            col = lax.broadcasted_iota(jnp.int32, diag.shape, 1)
            diag = jnp.where(col <= row, diag, NEG)
            top = jnp.max(diag, axis=1, keepdims=True)
            if i > 0:
                off = s[:, : i * block]
                top = jnp.maximum(top, jnp.max(off, axis=1, keepdims=True))
                e_ref[here, : i * block] = jnp.exp2(off - top).astype(bf16)
            e_ref[here, i * block : wide] = jnp.exp2(diag - top).astype(bf16)

    wait_all(vs.at[:, pl.ds(0, HEAD_DIM)], in_recv.at[2])

    for i in range(n_blocks):
        wide = (i + 1) * block

        @pl.loop(0, n_tiles)
        def _(r, i=i, wide=wide):
            here = pl.ds(pl.multiple_of(i * block + r * tile, tile), tile)
            both = dot(e_ref[here, :wide], vs[:wide, :])
            inv = 1.0 / both[:, HEAD_DIM:]
            out = both[:, :HEAD_DIM] * inv
            inv_ref[here, :] = inv
            o_ref[here, :] = out
            at_ref[here, :] = out.astype(bf16)

    def give_back(src, dst, send, recv, first=0, last=n_seq):
        @pl.loop(max(first, 1), last)
        def _(n):
            p = peer_of(n_seq - n)
            pltpu.make_async_remote_copy(
                src_ref=src.at[rows(p), :],
                dst_ref=dst.at[:, cols(me)],
                send_sem=send,
                recv_sem=recv,
                device_id={"seq": p},
                device_id_type=MESH,
            ).start()

        if first == 0:
            pltpu.make_async_copy(src.at[rows(me), :], dst.at[:, cols(me)], recv).start()

    give_back(at_ref, home_ref, out_send.at[0], out_recv.at[0])

    wait_all(gs, in_recv.at[3])

    @pl.loop(0, total // HEAD_DIM)
    def _(t):
        here = pl.ds(pl.multiple_of(t * HEAD_DIM, HEAD_DIM), HEAD_DIM)
        inv = inv_ref[here, :]
        gt_ref[:, here] = (gs[here, :].astype(f32) * inv).T.astype(bf16)
        qt_ref[:, here] = (qs[here, :].astype(f32) * (inv * scale)).T.astype(bf16)

    for j in range(n_blocks):
        lo = j * block
        res = dot(gt_ref[:, lo:], e_ref[lo:, lo : lo + block])
        dv_ref[lo : lo + block, :] = res.T.astype(bf16)
    give_back(dv_ref, dv_out.at[0], out_send.at[1], out_recv.at[1])

    for i in range(n_blocks):
        wide = (i + 1) * block

        @pl.loop(0, n_tiles)
        def _(r, i=i, wide=wide):
            here = pl.ds(pl.multiple_of(i * block + r * tile, tile), tile)
            g = gs[here, :]
            mean = jnp.sum(g.astype(f32) * o_ref[here, :], axis=1, keepdims=True)
            dprob = dot_t(g, vs[:wide, :HEAD_DIM])
            ds = (e_ref[here, :wide].astype(f32) * (dprob - mean)).astype(bf16)
            e_ref[here, :wide] = ds
            dq = dot(ds, ks[:wide, :]) * (inv_ref[here, :] * scale)
            dq_ref[here, :] = dq.astype(bf16)

    wait_all(home_ref, out_recv.at[0])
    attn = home_ref[...].astype(f32)
    blend_out[0] = jnp.where(live, rate * attn, 0.0).astype(bf16)
    dotted = jnp.sum(c_ref[...].astype(f32) * attn, axis=1, keepdims=True)
    lg = jnp.where(live, dotted * rate * (1.0 - rate), 0.0)
    eye = lax.broadcasted_iota(jnp.int32, (cap, cap), 0) == lax.broadcasted_iota(
        jnp.int32, (cap, cap), 1
    )
    lg_ref[...] = jnp.sum(jnp.where(eye, lg, 0.0), axis=0, keepdims=True)
    part = jnp.sum(lg * x_ref[...].astype(f32), axis=0, keepdims=True)
    for p in range(n_seq):
        part_ref[p] = part[:, p * HEAD_DIM : (p + 1) * HEAD_DIM]

    spread(
        lambda p: part_ref.at[pl.ds(p, 1)],
        part_in.at[pl.ds(me, 1)],
        sum_send.at[0],
        sum_recv.at[0],
        sum_recv.at[0],
    )
    give_back(dq_ref, dq_out.at[0], out_send.at[2], out_recv.at[2])

    for j in range(n_blocks):
        lo = j * block
        res = dot(qt_ref[:, lo:], e_ref[lo:, lo : lo + block])
        dk_ref[lo : lo + block, :] = res.T.astype(bf16)
    wait_all(part_in, sum_recv.at[0])
    count_sum = jnp.sum(part_in[...], axis=0, keepdims=True)
    dp_in[pl.ds(dp, 1)] = count_sum

    @pl.loop(1, n_dp)
    def _(n):
        pltpu.make_async_remote_copy(
            src_ref=dp_in.at[pl.ds(dp, 1)],
            dst_ref=dp_in.at[pl.ds(dp, 1)],
            send_sem=sum_send.at[1],
            recv_sem=sum_recv.at[1],
            device_id={"dp": lax.rem(dp + n, n_dp)},
            device_id_type=MESH,
        ).start()

    give_back(dk_ref, dk_out.at[0], out_send.at[3], out_recv.at[3], 0, n_seq // 2)
    wait_all(dp_in.at[pl.ds(0, n_dp - 1)], sum_recv.at[1])
    full_ref[pl.ds(me, 1)] = jnp.sum(dp_in[...], axis=0, keepdims=True)

    @pl.loop(1, n_seq)
    def _(n):
        pltpu.make_async_remote_copy(
            src_ref=full_ref.at[pl.ds(me, 1)],
            dst_ref=full_ref.at[pl.ds(me, 1)],
            send_sem=sum_send.at[2],
            recv_sem=sum_recv.at[2],
            device_id={"seq": peer_of(n)},
            device_id_type=MESH,
        ).start()

    give_back(dk_ref, dk_out.at[0], out_send.at[3], out_recv.at[3], n_seq // 2, n_seq)

    wait_all(full_ref.at[pl.ds(0, n_seq - 1)], sum_recv.at[2])
    for p in range(n_seq):
        rg_ref[:, p * HEAD_DIM : (p + 1) * HEAD_DIM] = full_ref[p]

    sent = pl.ds(0, total - cap)
    most = pl.ds(0, n_seq - 1)
    for a in range(4):
        wait_all(ks.at[sent, :], in_send.at[a])
    wait_all(counts.at[most], in_send.at[4])
    wait_all(counts.at[most], sum_send.at[0])
    wait_all(dp_in.at[pl.ds(0, n_dp - 1)], sum_send.at[1])
    wait_all(counts.at[most], sum_send.at[2])
    for a in range(3):
        wait_all(ks.at[sent, :], out_send.at[a])
    wait_all(dv_out, out_recv.at[1])
    wait_all(dq_out, out_recv.at[2])
    wait_all(ks.at[sent, :], out_send.at[3])
    wait_all(dk_out, out_recv.at[3])


def write_out(n, *refs):
    sems = refs[2 * n]
    copies = [pltpu.make_async_copy(refs[a], refs[n + a], sems.at[a]) for a in range(n)]
    for a, copy in enumerate(copies):
        copy.start(priority=a % 2)
    for copy in copies:
        copy.wait()


def body(x_rows, router_weight, query_rows, key_rows, value_rows, cotangent, picked):
    n_seq = lax.axis_size("seq")
    n_dp = lax.axis_size("dp")
    _, cap, width = x_rows.shape
    total = n_seq * cap
    block = min(512, total // 2)
    tile = 128
    f32 = jnp.float32
    bf16 = jnp.bfloat16
    anyspace = pl.BlockSpec(memory_space=pl.ANY)
    hbm = pl.BlockSpec(memory_space=pltpu.HBM)
    vmem = pl.BlockSpec(memory_space=pltpu.VMEM)
    big = pltpu.VMEM(x_rows.shape, bf16)
    head = pltpu.VMEM((total, HEAD_DIM), bf16)
    headf = pltpu.VMEM((total, HEAD_DIM), f32)
    own = pltpu.VMEM((cap, width), bf16)
    chunks = pltpu.VMEM((n_seq, 1, HEAD_DIM), f32)
    out = pl.pallas_call(
        functools.partial(kernel, n_seq, n_dp, block, tile),
        out_shape=(
            big,
            big,
            big,
            big,
            pltpu.VMEM((1, cap), f32),
            pltpu.VMEM((1, width), f32),
        ),
        in_specs=[hbm] * 7,
        out_specs=(vmem,) * 6,
        scratch_shapes=[
            own,
            own,
            pltpu.VMEM((1, width), f32),
            pltpu.VMEM((1, cap), jnp.int32),
            own,
            pltpu.VMEM((1, 1, HEAD_DIM), f32),
            chunks,
            pltpu.VMEM((1, total), f32),
            head,
            head,
            pltpu.VMEM((total, 2 * HEAD_DIM), bf16),
            head,
            pltpu.VMEM((total, total), bf16),
            headf,
            headf,
            head,
            head,
            head,
            head,
            pltpu.VMEM((HEAD_DIM, total), bf16),
            pltpu.VMEM((HEAD_DIM, total), bf16),
            own,
            chunks,
            chunks,
            pltpu.VMEM((n_dp, 1, HEAD_DIM), f32),
            chunks,
            pltpu.SemaphoreType.DMA((5,)),
            pltpu.SemaphoreType.DMA((5,)),
            pltpu.SemaphoreType.DMA((4,)),
            pltpu.SemaphoreType.DMA((4,)),
            pltpu.SemaphoreType.DMA((3,)),
            pltpu.SemaphoreType.DMA((3,)),
            pltpu.SemaphoreType.DMA((4,)),
        ],
        compiler_params=pltpu.CompilerParams(
            collective_id=0, has_side_effects=True, vmem_limit_bytes=48 * 1024 * 1024
        ),
    )(
        *(
            pltpu.with_memory_space_constraint(a, pltpu.HBM)
            for a in (
                x_rows,
                router_weight.reshape(1, width),
                query_rows,
                key_rows,
                value_rows,
                cotangent,
                picked,
            )
        )
    )
    blended, grad_q, grad_k, grad_v, logit_grad, router_grad = pl.pallas_call(
        functools.partial(write_out, len(out)),
        out_shape=tuple(pltpu.HBM(o.shape, o.dtype) for o in out),
        in_specs=[vmem] * len(out),
        out_specs=(hbm,) * len(out),
        scratch_shapes=[pltpu.SemaphoreType.DMA((len(out),))],
        compiler_params=pltpu.CompilerParams(vmem_limit_bytes=16 * 1024 * 1024),
    )(*out)
    return blended, grad_q, grad_k, grad_v, logit_grad, router_grad.reshape(width)


def solution(mesh):
    row3 = P("dp", "seq", None)
    row2 = P("dp", "seq")
    mapped = jax.shard_map(
        body,
        mesh=mesh,
        in_specs=(row3, P(), row3, row3, row3, row3, row2),
        out_specs=(row3, row3, row3, row3, row2, P()),
        check_vma=False,
    )

    def run(
        x_rows,
        router_weight,
        query_rows,
        key_rows,
        value_rows,
        cotangent,
        picked,
        dest_owner,
        dest_slot,
    ):
        return mapped(
            x_rows, router_weight, query_rows, key_rows, value_rows, cotangent, picked
        )

    return run
```
